32 devices in a mesh: grp: 4 (over z), gx: 2 (over y), gy: 4 (over x, core).
Axes of the slice: x: 2, y: 2, z: 4, core: 2. Of those that a mesh axis runs over, the one named last changes fastest.
Arguments:
- states: bfloat16 [12, 32, 64, 512], P(None, 'gx', 'gy', 'grp'), may hold values from 0 to 1
- membrane: float32 [32, 64, 512], P('gx', 'gy', 'grp'), may hold values from -3 to 3
- phi_heart: float32 [32, 64, 512], P('gx', 'gy', 'grp'), may hold values from -3 to 3
- ion_params: float32 [5, 12], replicated, may hold values from -1.5 to 20, as said below
- torso_phi: float32 [32, 128, 512], P('gx', 'gy', 'grp'), may hold values from -3 to 3
- tissue_scale: float32 [32, 128, 512], P('gx', 'gy', 'grp'), may hold values from 0.5 to 2
- labels: int32 [32, 128, 512], P('gx', 'gy', 'grp'), may hold values from 0 to 3
- cond_table: float32 [4], replicated, may hold values from 0.1 to 2
- send_node: int32 [4, 2, 4, 8, 512], P('grp', 'gx', 'gy'), may hold values from 0 to 8191
- send_count: int32 [4, 2, 4, 8], P('grp', 'gx', 'gy'), may hold values from 64 to 512, as said below
- recv_voxel: int32 [4, 2, 4, 8, 512], P('grp', 'gx', 'gy'), may hold values from 0 to 16383
- recv_count: int32 [4, 2, 4, 8], P('grp', 'gx', 'gy'), may hold values from 64 to 512, as said below
Outputs:
- new_membrane: float32 [32, 64, 512], P('gx', 'gy', 'grp')
- heart_phi: float32 [32, 64, 512], P('gx', 'gy', 'grp')
- torso_out: float32 [32, 128, 512], P('gx', 'gy', 'grp')
The draws below stay inside these ranges and needn't reach their ends.
Inputs may be any that keep to these rules, and one draw needn't show every extreme that they name: `ion_params`: rows are midpoints in -1 to 1, slopes in 0.1 to 0.5, relaxation rates in 0.5 to 20, conductances in 0.1 to 0.6 and reversal potentials in -1.5 to 1.5, one column per state. send_count[g, i, j, p] is the number of live slots, from the first on, of the patch that device (g, i, j) sends to peer p of its slab; every device sends exactly 512 to one peer. recv_count[g, i, j, s] equals send_count of peer s of slab g for peer i * 4 + j; every device receives exactly 512 from one peer.
All inputs are finite; a program needn't handle non-finite values.
Results may differ from the reference program's by a relative error of at most 0.0003.
Values sent between devices are 32-bit elements; how exact they have to be, the bound alone decides.
A program may use at most 128 MiB of HBM per device.

```python
import math
import jax
import jax.numpy as jnp

STATES = 12
LABELS = 4
SWEEPS_H = 3
SWEEPS_T = 4
CAP = 512
HX = 16
HY = 16
HZ = 128
TX = 16
TY = 32
TZ = 128
PEERS = 8
HNODES = 32768
TVOX = 65536
NHX = 32
NHY = 64
NHZ = 512
NTX = 32
NTY = 128
NTZ = 512
N_GRP = 4
N_GX = 2
N_GY = 4


def one_perm(subkey):
    return jax.random.permutation(subkey, PEERS).astype(jnp.int32)


def pair_counts(key):
    base_key = jax.random.fold_in(key, 7)
    key_hi, key_base, key_perm = jax.random.split(base_key, 3)
    ceiling = jax.random.randint(key_hi, (N_GRP, 1, PEERS), CAP // 4, CAP + 1)
    counts = jax.random.randint(key_base, (N_GRP, PEERS, PEERS), ceiling // 2, ceiling + 1)
    chosen = jax.vmap(one_perm)(jax.random.split(key_perm, N_GRP))
    full_pair = jnp.arange(PEERS, dtype=jnp.int32)[None, None, :] == chosen[:, :, None]
    return jnp.where(full_pair, CAP, counts).astype(jnp.int32)


def draw_send_count(key, part):
    return pair_counts(key).reshape(N_GRP, N_GX, N_GY, PEERS)


def draw_recv_count(key, part):
    return pair_counts(key).transpose(0, 2, 1).reshape(N_GRP, N_GX, N_GY, PEERS)


def draw_ion_params(key, part):
    subkeys = jax.random.split(jax.random.fold_in(key, 11), 5)
    midpoint = jax.random.uniform(subkeys[0], (STATES,), jnp.float32, -1.0, 1.0)
    steepness = jax.random.uniform(subkeys[1], (STATES,), jnp.float32, 0.1, 0.5)
    relax_rate = jnp.exp(jax.random.uniform(subkeys[2], (STATES,), jnp.float32, jnp.log(0.5), jnp.log(20.0)))
    conductance = jax.random.uniform(subkeys[3], (STATES,), jnp.float32, 0.1, 0.6)
    reversal = jax.random.uniform(subkeys[4], (STATES,), jnp.float32, -1.5, 1.5)
    return jnp.stack([midpoint, steepness, relax_rate, conductance, reversal]).astype(jnp.float32)


def plant(result, own_key, smallest, high):
    longest = result.shape.index(max(result.shape))
    spots = []
    for shift in (0, 1):
        where = [jax.random.randint(jax.random.fold_in(own_key, axis), (), 0, length) for axis, length in enumerate(result.shape)]
        where[longest] = (where[longest] + shift) % result.shape[longest]
        spots.append(tuple(where))
    return result.at[spots[0]].set(smallest).at[spots[1]].set(high)


def levels(own_key, dims, pieces, smallest, top_value):
    factor_of = 1.0
    for position, shards_of in pieces:
        draws = jax.random.uniform(jax.random.fold_in(jax.random.fold_in(own_key, 6), position), (shards_of,), jnp.float32, smallest / len(pieces), top_value / len(pieces))
        factor_of = factor_of * jnp.repeat(jnp.exp(draws), dims[position] // shards_of).reshape((-1,) + (1,) * (len(dims) - 1 - position))
    return factor_of


def bell_draw(own_key, shape, scale, reach, pieces=(), kind=jnp.bfloat16):
    factor_of = levels(own_key, shape, pieces, -0.22, 0.18) if pieces else 1.0
    drawn = jax.random.normal(own_key, shape, jnp.float32) * scale * factor_of
    return jnp.minimum(jnp.maximum(drawn, -reach), reach).astype(kind)


def setup_inputs(seed: int = 0) -> dict:
    keys = jax.random.split(jax.random.key(seed), 13)
    return {
        "states": jnp.clip(1.0 * jax.random.uniform(keys[0], (STATES, NHX, NHY, NHZ), jnp.float32) ** levels(keys[0], (STATES, NHX, NHY, NHZ), ((1, 2), (2, 4), (3, 4)), -0.2, 0.2), 0.0, 1.0).astype(jnp.bfloat16),
        "membrane": bell_draw(keys[1], (NHX, NHY, NHZ), 0.5, 3.0, ((0, 2), (1, 4), (2, 4)), jnp.float32),
        "phi_heart": bell_draw(keys[2], (NHX, NHY, NHZ), 0.5, 3.0, ((0, 2), (1, 4), (2, 4)), jnp.float32),
        "ion_params": draw_ion_params(jax.random.fold_in(keys[12], 71), 0),
        "torso_phi": bell_draw(keys[4], (NTX, NTY, NTZ), 0.5, 3.0, ((0, 2), (1, 4), (2, 4)), jnp.float32),
        "tissue_scale": jnp.clip(jnp.exp(math.log(2.0) - 1.3862944 * jax.random.uniform(keys[5], (NTX, NTY, NTZ), jnp.float32) ** levels(keys[5], (NTX, NTY, NTZ), ((0, 2), (1, 4), (2, 4)), -0.2, 0.2)), 0.5, 2.0),
        "labels": plant(jax.random.randint(keys[6], (NTX, NTY, NTZ), 0, LABELS), jax.random.fold_in(keys[6], 1), 0, LABELS - 1).astype(jnp.int32),
        "cond_table": jnp.clip(jnp.exp(jax.random.uniform(keys[7], (LABELS,), jnp.float32, math.log(0.1), math.log(2.0))), 0.1, 2.0),
        "send_node": plant(jax.random.randint(keys[8], (N_GRP, N_GX, N_GY, PEERS, CAP), 0, HNODES // 4), jax.random.fold_in(keys[8], 1), 0, (HNODES // 4) - 1).astype(jnp.int32),
        "send_count": draw_send_count(jax.random.fold_in(keys[12], 71), 0),
        "recv_voxel": plant(jax.random.randint(keys[10], (N_GRP, N_GX, N_GY, PEERS, CAP), 0, TVOX // 4), jax.random.fold_in(keys[10], 1), 0, (TVOX // 4) - 1).astype(jnp.int32),
        "recv_count": draw_recv_count(jax.random.fold_in(keys[12], 71), 0),
    }


time_step = 0.1
intra_cond = 0.25
extra_cond = 0.5
penalty = 2.0
cheb_low = 0.1
cheb_high = 2.0


def cheb_coeffs(sweeps):
    centre = 0.5 * (cheb_high + cheb_low)
    half_width = 0.5 * (cheb_high - cheb_low)
    scaled = centre / half_width
    coeffs = [(0.0, 1.0 / centre)]
    rho_old = 1.0 / scaled
    for number in range(1, sweeps):
        rho_new = 1.0 / (2.0 * scaled - rho_old)
        coeffs.append((rho_new * rho_old, 2.0 * rho_new / half_width))
        rho_old = rho_new
    return coeffs


def face_mask(cell_count, margin, start_at, whole):
    positions = start_at + jnp.arange(cell_count + 2 * margin, dtype=jnp.int32) - margin
    return ((positions >= 0) & (positions + 1 <= whole - 1)).astype(jnp.float32)


def harmonic(lower_cell, upper_cell):
    return 2.0 * lower_cell * upper_cell / (lower_cell + upper_cell)


def faces_from(conduct, mask_x, mask_y, mask_z):
    face_x = jnp.concatenate([harmonic(conduct[:-1], conduct[1:]), jnp.zeros_like(conduct[:1])], 0) * mask_x[:, None, None]
    face_y = jnp.concatenate([harmonic(conduct[:, :-1], conduct[:, 1:]), jnp.zeros_like(conduct[:, :1])], 1) * mask_y[None, :, None]
    face_z = jnp.concatenate([harmonic(conduct[:, :, :-1], conduct[:, :, 1:]), jnp.zeros_like(conduct[:, :, :1])], 2) * mask_z[None, None, :]
    return face_x, face_y, face_z


def flux_sum(values, conductances):
    face_x, face_y, face_z = conductances
    along_x = face_x[:-1] * (values[1:] - values[:-1])
    along_y = face_y[:, :-1] * (values[:, 1:] - values[:, :-1])
    along_z = face_z[:, :, :-1] * (values[:, :, 1:] - values[:, :, :-1])
    summed = (along_x[:-1] - along_x[1:])[:, 1:-1, 1:-1]
    summed = summed + (along_y[:, :-1] - along_y[:, 1:])[1:-1, :, 1:-1]
    return summed + (along_z[:, :, :-1] - along_z[:, :, 1:])[1:-1, 1:-1, :]


def face_total(conductances):
    face_x, face_y, face_z = conductances
    summed = (face_x[:-2] + face_x[1:-1])[:, 1:-1, 1:-1]
    summed = summed + (face_y[:, :-2] + face_y[:, 1:-1])[1:-1, :, 1:-1]
    return summed + (face_z[:, :, :-2] + face_z[:, :, 1:-1])[1:-1, 1:-1, :]


def lookup(labels, cond_table):
    picked = jnp.zeros(labels.shape, jnp.float32)
    for number in range(LABELS):
        picked = picked + jnp.where(labels == number, cond_table[number], jnp.zeros((), jnp.float32))
    return picked


def ionic_current(states, membrane, ion_params):
    params_col = ion_params[:, :, None, None, None]
    gate_vals = states.astype(jnp.float32)
    voltage = membrane[None]
    steady = jax.nn.sigmoid((voltage - params_col[0]) / params_col[1])
    gate_vals = steady + (gate_vals - steady) * jnp.exp(-time_step * params_col[2])
    return jnp.sum(params_col[3] * gate_vals * (voltage - params_col[4]), axis=0)


def padded(values):
    return jnp.pad(values, 1, mode="wrap")


def global_faces(conduct_ext, grid_shape):
    mask_x = jnp.ones((grid_shape[0] + 2,), jnp.float32)
    mask_y = face_mask(grid_shape[1], 1, 0, grid_shape[1])
    mask_z = face_mask(grid_shape[2], 1, 0, grid_shape[2])
    return faces_from(conduct_ext, mask_x, mask_y, mask_z)


def to_blocks(values, size_x, size_y, size_z):
    blocks = values.reshape(N_GX, size_x, N_GY, size_y, N_GRP, size_z).transpose(4, 0, 2, 1, 3, 5)
    return blocks.reshape(N_GRP, N_GX * N_GY, size_x * size_y * size_z)


def from_blocks(blocks, size_x, size_y, size_z):
    values = blocks.reshape(N_GRP, N_GX, N_GY, size_x, size_y, size_z).transpose(1, 3, 2, 4, 0, 5)
    return values.reshape(N_GX * size_x, N_GY * size_y, N_GRP * size_z)


def reference(states, membrane, phi_heart, ion_params, torso_phi, tissue_scale, labels, cond_table, send_node, send_count, recv_voxel, recv_count):
    heart_shape = membrane.shape
    torso_shape = torso_phi.shape
    unit_faces = global_faces(jnp.ones((heart_shape[0] + 2, heart_shape[1] + 2, heart_shape[2] + 2), jnp.float32), heart_shape)
    heart_total = (intra_cond + extra_cond) * face_total(unit_faces)
    lap_membrane = flux_sum(padded(membrane), unit_faces)
    source = -intra_cond * lap_membrane
    iterate = phi_heart
    update = jnp.zeros_like(iterate)
    for carry_coef, resid_coef in cheb_coeffs(SWEEPS_H):
        residue = (source - (intra_cond + extra_cond) * flux_sum(padded(iterate), unit_faces)) / heart_total
        update = carry_coef * update + resid_coef * residue
        iterate = iterate + update
    phi_new = iterate
    current = ionic_current(states, membrane, ion_params)
    lap_phi = flux_sum(padded(phi_new), unit_faces)
    new_membrane = membrane + time_step * (-intra_cond * (lap_membrane + lap_phi) - current)

    peer_count = N_GX * N_GY
    slot_ids = jnp.arange(CAP, dtype=jnp.int32)
    slab_ids = jnp.arange(N_GRP, dtype=jnp.int32)[:, None, None, None]
    peer_ids = jnp.arange(peer_count, dtype=jnp.int32)[None, :, None, None]
    sender_live = slot_ids[None, None, None, :] < send_count.reshape(N_GRP, peer_count, peer_count)[..., None]
    heart_index = (slab_ids * peer_count + peer_ids) * HNODES + send_node.reshape(N_GRP, peer_count, peer_count, CAP).astype(jnp.int32)
    heart_flat = to_blocks(phi_new, HX, HY, HZ).reshape(-1)
    sent_vals = jnp.where(sender_live, heart_flat[heart_index], jnp.zeros((), jnp.float32))
    arrived = sent_vals.transpose(0, 2, 1, 3)
    receiver_live = slot_ids[None, None, None, :] < recv_count.reshape(N_GRP, peer_count, peer_count)[..., None]
    torso_index = (slab_ids * peer_count + peer_ids) * TVOX + recv_voxel.reshape(N_GRP, peer_count, peer_count, CAP).astype(jnp.int32)
    live_weight = receiver_live.astype(jnp.float32) * penalty
    right_side = jnp.zeros((N_GRP * peer_count * TVOX,), jnp.float32).at[torso_index.reshape(-1)].add((live_weight * arrived).reshape(-1))
    weight = jnp.zeros((N_GRP * peer_count * TVOX,), jnp.float32).at[torso_index.reshape(-1)].add(live_weight.reshape(-1))
    right_side = from_blocks(right_side.reshape(N_GRP, peer_count, TVOX), TX, TY, TZ)
    weight = from_blocks(weight.reshape(N_GRP, peer_count, TVOX), TX, TY, TZ)

    conduct = tissue_scale * lookup(labels, cond_table)
    conductances = global_faces(padded(conduct), torso_shape)
    diagonal = face_total(conductances) + weight
    iterate = torso_phi
    update = jnp.zeros_like(iterate)
    for carry_coef, resid_coef in cheb_coeffs(SWEEPS_T):
        residue = (right_side - (flux_sum(padded(iterate), conductances) + weight * iterate)) / diagonal
        update = carry_coef * update + resid_coef * residue
        iterate = iterate + update
    torso_out = iterate

    torso_flat = to_blocks(torso_out, TX, TY, TZ).reshape(-1)
    returned = jnp.where(receiver_live, penalty * (arrived - torso_flat[torso_index]), jnp.zeros((), jnp.float32))
    came_back = returned.transpose(0, 2, 1, 3)
    flux_in = jnp.zeros((N_GRP * peer_count * HNODES,), jnp.float32).at[heart_index.reshape(-1)].add(jnp.where(sender_live, came_back, jnp.zeros((), jnp.float32)).reshape(-1))
    flux_in = from_blocks(flux_in.reshape(N_GRP, peer_count, HNODES), HX, HY, HZ)
    heart_phi = phi_new - flux_in / heart_total
    return new_membrane, heart_phi, torso_out
```

```python
import functools

import jax
import jax.numpy as jnp
from jax import lax
from jax.experimental import pallas as pl
from jax.experimental.pallas import tpu as pltpu
from jax.sharding import PartitionSpec as P

LABELS = 4
SWEEPS_H = 3
SWEEPS_T = 4

time_step = 0.1
intra_cond = 0.25
extra_cond = 0.5
penalty = 2.0
cheb_low = 0.1
cheb_high = 2.0

MESH = pl.DeviceIdType.MESH
F32 = jnp.float32
BF16 = jnp.bfloat16


def cheb_coeffs(sweeps):
    centre = 0.5 * (cheb_high + cheb_low)
    half_width = 0.5 * (cheb_high - cheb_low)
    scaled = centre / half_width
    coeffs = [(0.0, 1.0 / centre)]
    rho_old = 1.0 / scaled
    for number in range(1, sweeps):
        rho_new = 1.0 / (2.0 * scaled - rho_old)
        coeffs.append((rho_new * rho_old, 2.0 * rho_new / half_width))
        rho_old = rho_new
    return coeffs


def harmonic(a, b):
    return 2.0 * a * b / (a + b)


def two_terms(values):
    high = values.astype(BF16)
    return high, (values - high.astype(F32)).astype(BF16)


class Grid:
    def __init__(self, shape, stage, landing, sends, recvs, ypad, place):
        self.shape = shape
        self.stage = stage
        self.landing = landing
        self.sends = sends
        self.recvs = recvs
        self.ypad = ypad
        self.place = place

    def clear_ends(self):
        for axis, (_, low, high) in enumerate(self.place):
            for side, (_, present) in enumerate((low, high)):
                if present is None:
                    continue

                @pl.when(jnp.logical_not(present))
                def _(axis=axis, side=side):
                    ref = self.landing[axis]
                    ref[side] = jnp.zeros(ref.shape[1:], F32)

    def pack(self, slot, field):
        nx, ny, nz = self.shape
        xs, ys, zs = self.stage
        xs[0, slot] = field[0]
        xs[1, slot] = field[nx - 1]
        ys[0, slot] = field[:, 0:1, :]
        ys[1, slot] = field[:, ny - 1 : ny, :]
        turned = jnp.transpose(field.reshape(nx * ny, nz))
        zs[0, slot] = turned[0:1, :]
        zs[1, slot] = turned[nz - 1 : nz, :]

    def copies(self, turn, first, count):
        for axis, (name, low, high) in enumerate(self.place):
            for side, there in enumerate((low, high)):
                back = (high, low)[side]
                yield (
                    pltpu.make_async_remote_copy(
                        src_ref=self.stage[axis].at[side, pl.ds(first, count)],
                        dst_ref=self.landing[axis].at[1 - side, pl.ds(first, count)],
                        send_sem=self.sends.at[turn, axis, side],
                        recv_sem=self.recvs.at[turn, axis, 1 - side],
                        device_id={name: there[0]},
                        device_id_type=MESH,
                    ),
                    there[1],
                    back[1],
                )

    def send(self, turn, first, count):
        for copy, out, _ in self.copies(turn, first, count):
            if out is None:
                copy.start()
            else:
                pl.when(out)(copy.start)

    def wait(self, turn, first, count):
        for copy, _, back in self.copies(turn, first, count):
            if back is None:
                copy.wait_recv()
            else:
                pl.when(back)(copy.wait_recv)

    def finish(self, turn, first, count):
        for copy, out, _ in self.copies(turn, first, count):
            if out is None:
                copy.wait_send()
            else:
                pl.when(out)(copy.wait_send)

    def around(self, slot, field):
        nx, ny, nz = self.shape
        rx, ry, rz = self.landing
        below_x = jnp.concatenate([rx[0, slot][None], field[:-1]], axis=0)
        above_x = jnp.concatenate([field[1:], rx[1, slot][None]], axis=0)
        self.ypad[:, 8 : 8 + ny, :] = field
        self.ypad[:, 7:8, :] = ry[0, slot]
        self.ypad[:, 8 + ny : 9 + ny, :] = ry[1, slot]
        below_y = self.ypad[:, 7 : 7 + ny, :]
        above_y = self.ypad[:, 9 : 9 + ny, :]
        depth = lax.broadcasted_iota(jnp.int32, (nz, nx * ny), 0)
        ends = jnp.transpose(jnp.where(depth == 0, rz[0, slot], rz[1, slot]))
        flat = field.reshape(nx * ny, nz)
        lanes = lax.broadcasted_iota(jnp.int32, (nx * ny, nz), 1)
        below_z = jnp.where(lanes == 0, ends, pltpu.roll(flat, 1, 1)).reshape(nx, ny, nz)
        above_z = jnp.where(lanes == nz - 1, ends, pltpu.roll(flat, nz - 1, 1)).reshape(nx, ny, nz)
        return below_x, above_x, below_y, above_y, below_z, above_z


def spots(node_ref, count_ref, peer, rows, width):
    index = node_ref[pl.ds(peer, 1), :]
    cap = index.shape[1]
    slot_ids = lax.broadcasted_iota(jnp.int32, (1, cap), 1)
    index = jnp.where(slot_ids < count_ref[peer], index, -1)
    row_ids = lax.broadcasted_iota(jnp.int32, (rows, cap), 0)
    col_ids = lax.broadcasted_iota(jnp.int32, (width, cap), 0)
    row_hot = jnp.where(row_ids == lax.shift_right_arithmetic(index, 7), 1.0, 0.0).astype(BF16)
    return row_hot, col_ids == (index & (width - 1))


def turned_table(layer, rows, width):
    high, low = two_terms(jnp.transpose(layer.reshape(rows, width)))
    return jnp.concatenate([high, low], axis=1)


def pick(table, row_hot, col_hot):
    chosen = jnp.dot(
        table, jnp.concatenate([row_hot, row_hot], axis=0), preferred_element_type=F32
    )
    return jnp.sum(jnp.where(col_hot, chosen, 0.0), axis=0, keepdims=True)


def place_at(values, row_hot, col_hot):
    high = values.astype(BF16).astype(F32)
    low = values - high
    columns = jnp.concatenate(
        [jnp.where(col_hot, high, 0.0).astype(BF16), jnp.where(col_hot, low, 0.0).astype(BF16)],
        axis=0,
    )
    return lax.dot_general(
        row_hot, columns, (((1,), (1,)), ((), ())), preferred_element_type=F32
    )


def kernel(
    sizes,
    states,
    membrane,
    phi_heart,
    ion_params,
    torso_phi,
    tissue_scale,
    labels,
    cond_table,
    send_node,
    send_count,
    recv_voxel,
    recv_count,
    new_membrane,
    heart_phi,
    torso_out,
    hsx, hsy, hsz, hrx, hry, hrz, hypad, hsend, hrecv,
    tsx, tsy, tsz, trx, try_, trz, typad, tsend, trecv,
    sent, arrived, returned, came,
    out_sem, in_sem, back_sem, home_sem,
    update_h, source_h, current_h, gains, update_t, right_t, weight_t, flux_h,
):
    n_grp, n_gx, n_gy = sizes
    peers = n_gx * n_gy
    unroll = peers <= 8
    g = lax.axis_index("grp")
    i = lax.axis_index("gx")
    j = lax.axis_index("gy")
    me = i * n_gy + j
    hshape = membrane.shape
    tshape = torso_phi.shape
    place = (
        ("gx", (lax.rem(i + n_gx - 1, n_gx), None), (lax.rem(i + 1, n_gx), None)),
        ("gy", (jnp.maximum(j - 1, 0), j > 0), (jnp.minimum(j + 1, n_gy - 1), j < n_gy - 1)),
        ("grp", (jnp.maximum(g - 1, 0), g > 0), (jnp.minimum(g + 1, n_grp - 1), g < n_grp - 1)),
    )
    heart = Grid(hshape, (hsx, hsy, hsz), (hrx, hry, hrz), hsend, hrecv, hypad, place)
    torso = Grid(tshape, (tsx, tsy, tsz), (trx, try_, trz), tsend, trecv, typad, place)

    heart.clear_ends()
    torso.clear_ends()

    def peer_at(step):
        other = lax.rem(me + step, peers)
        return other, {"gx": other // n_gy, "gy": lax.rem(other, n_gy)}

    barrier = pltpu.get_barrier_semaphore()

    def greet(step, carry):
        pl.semaphore_signal(barrier, inc=1, device_id=peer_at(step)[1], device_id_type=MESH)
        return carry

    lax.fori_loop(1, peers, greet, 0, unroll=unroll)
    _, low_z, high_z = place[2]
    for there, present in (low_z, high_z):

        @pl.when(present)
        def _(there=there):
            pl.semaphore_signal(barrier, inc=1, device_id={"grp": there}, device_id_type=MESH)

    heart.pack(0, membrane[...])
    heart.pack(1, phi_heart[...])
    names = labels[...]
    table = jnp.where(names == 0, cond_table[0], 0.0)
    for number in range(1, LABELS):
        table = jnp.where(names == number, cond_table[number], table)
    conduct = tissue_scale[...] * table
    torso.pack(0, conduct)
    torso.pack(1, torso_phi[...])

    pl.semaphore_wait(
        barrier, peers - 1 + (g > 0).astype(jnp.int32) + (g < n_grp - 1).astype(jnp.int32)
    )
    heart.send(0, 0, 2)
    torso.send(0, 0, 2)

    voltage = membrane[...]
    current = jnp.zeros(hshape, F32)
    for state in range(states.shape[0]):
        line = jnp.zeros((1, 1, hshape[2]), F32)
        half_slope = 0.5 / (line + ion_params[1, state])
        decay = jnp.exp(line - time_step * ion_params[2, state])
        steady = 0.5 + 0.5 * jnp.tanh((voltage - ion_params[0, state]) * half_slope)
        gate = steady + (states[state].astype(F32) - steady) * decay
        current = current + ion_params[3, state] * gate * (voltage - ion_params[4, state])
    current_h[...] = current

    ny = lax.broadcasted_iota(jnp.int32, hshape, 1) + j * hshape[1]
    nz = lax.broadcasted_iota(jnp.int32, hshape, 2) + g * hshape[2]
    diag = (
        6.0
        - jnp.where(ny == 0, 1.0, 0.0)
        - jnp.where(ny == hshape[1] * n_gy - 1, 1.0, 0.0)
        - jnp.where(nz == 0, 1.0, 0.0)
        - jnp.where(nz == hshape[2] * n_grp - 1, 1.0, 0.0)
    )
    inverse = 1.0 / diag

    def total_of(parts):
        return ((parts[0] + parts[1]) + (parts[2] + parts[3])) + (parts[4] + parts[5])

    heart.wait(0, 0, 2)
    lap_mem = diag * voltage - total_of(heart.around(0, voltage))
    source_h[...] = lap_mem
    base = (-intra_cond / (intra_cond + extra_cond)) * lap_mem * inverse
    iterate = phi_heart[...]
    update = None
    for number, (carry_coef, resid_coef) in enumerate(cheb_coeffs(SWEEPS_H)):
        if number > 0:
            heart.wait(number, number + 1, 1)
        around = total_of(heart.around(number + 1, iterate))
        residue = base - iterate + around * inverse
        update = resid_coef * residue if update is None else carry_coef * update + resid_coef * residue
        iterate = iterate + update
        heart.pack(number + 2, iterate)
        heart.send(number + 1, number + 2, 1)
        if number == 0:
            rows = tshape[0] // 4 * tshape[1]

            def weigh(peer, carry):
                row_hot, col_hot = spots(recv_voxel, recv_count, peer, rows, tshape[2])
                ones = jnp.where(col_hot, 1.0, 0.0).astype(BF16)
                return carry + lax.dot_general(
                    row_hot, ones, (((1,), (1,)), ((), ())), preferred_element_type=F32
                )

            weight_t[...] = penalty * lax.fori_loop(
                0, peers, weigh, jnp.zeros((rows, tshape[2]), F32), unroll=unroll
            )
    phi_new = iterate

    layer_h = hshape[0] // 4
    rows_h = layer_h * hshape[1]
    table_h = turned_table(phi_new[:layer_h], rows_h, hshape[2])

    def patch(step, source, target, sends, recvs):
        other, where = peer_at(step)
        return pltpu.make_async_remote_copy(
            src_ref=source.at[other],
            dst_ref=target.at[me],
            send_sem=sends.at[other],
            recv_sem=recvs.at[me],
            device_id=where,
            device_id_type=MESH,
        )

    def landed(step, source, target, sends, recvs):
        other, where = peer_at(step)
        return pltpu.make_async_remote_copy(
            src_ref=source.at[other],
            dst_ref=target.at[other],
            send_sem=sends.at[other],
            recv_sem=recvs.at[other],
            device_id=where,
            device_id_type=MESH,
        )

    def give(step, carry):
        other, _ = peer_at(step)
        row_hot, col_hot = spots(send_node, send_count, other, rows_h, hshape[2])
        sent[other] = pick(table_h, row_hot, col_hot)
        patch(step, sent, arrived, out_sem, in_sem).start()
        return carry

    lax.fori_loop(1, peers, give, 0, unroll=unroll)
    row_hot, col_hot = spots(send_node, send_count, me, rows_h, hshape[2])
    arrived[me] = pick(table_h, row_hot, col_hot)

    heart.wait(SWEEPS_H, SWEEPS_H + 1, 1)
    lap_phi = diag * phi_new - total_of(heart.around(SWEEPS_H + 1, phi_new))
    new_membrane[...] = voltage + time_step * (
        -intra_cond * (source_h[...] + lap_phi) - current_h[...]
    )
    update_h[...] = phi_new

    torso.wait(0, 0, 2)
    layer = tshape[0] // 4
    rows = layer * tshape[1]
    faces = [harmonic(conduct, other) for other in torso.around(0, conduct)]
    weight = weight_t[...].reshape(layer, tshape[1], tshape[2])
    total = total_of(faces)
    total = jnp.concatenate([total[:layer] + weight, total[layer:]], axis=0)
    scale = 1.0 / total
    for number in range(6):
        gains[number] = faces[number] * scale
    right_t[...] = penalty * scale[:layer]
    iterate = torso_phi[...]
    update_t[...] = -iterate + total_of(
        [gains[n] * other for n, other in enumerate(torso.around(1, iterate))]
    )

    def gather_right(step, carry):
        other, _ = peer_at(step)
        landed(step, sent, arrived, out_sem, in_sem).wait_recv()
        row_hot, col_hot = spots(recv_voxel, recv_count, other, rows, tshape[2])
        return carry + place_at(arrived[other], row_hot, col_hot)

    row_hot, col_hot = spots(recv_voxel, recv_count, me, rows, tshape[2])
    summed = place_at(arrived[me], row_hot, col_hot)
    summed = lax.fori_loop(1, peers, gather_right, summed, unroll=unroll)
    summed = summed[:, : tshape[2]] + summed[:, tshape[2] :]
    right = summed.reshape(layer, tshape[1], tshape[2]) * right_t[...]
    right_t[...] = right

    coeffs = cheb_coeffs(SWEEPS_T)
    update = update_t[...]
    update = coeffs[0][1] * jnp.concatenate([update[:layer] + right, update[layer:]], axis=0)
    iterate = iterate + update
    for number in range(1, SWEEPS_T):
        torso.pack(number + 1, iterate)
        torso.send(number, number + 1, 1)
        torso.wait(number, number + 1, 1)
        residue = -iterate + total_of(
            [gains[n] * other for n, other in enumerate(torso.around(number + 1, iterate))]
        )
        residue = jnp.concatenate([residue[:layer] + right_t[...], residue[layer:]], axis=0)
        update = coeffs[number][0] * update + coeffs[number][1] * residue
        iterate = iterate + update
    table_t = turned_table(iterate[:layer], rows, tshape[2])

    def give_back(step, carry):
        other, _ = peer_at(step)
        row_hot, col_hot = spots(recv_voxel, recv_count, other, rows, tshape[2])
        returned[other] = penalty * (arrived[other] - pick(table_t, row_hot, col_hot))
        patch(step, returned, came, back_sem, home_sem).start()
        return carry

    lax.fori_loop(1, peers, give_back, 0, unroll=unroll)
    row_hot, col_hot = spots(recv_voxel, recv_count, me, rows, tshape[2])
    came[me] = penalty * (arrived[me] - pick(table_t, row_hot, col_hot))
    torso_out[...] = iterate
    phi_new = update_h[...]
    heart_phi[...] = phi_new

    heart.finish(0, 0, 2)
    torso.finish(0, 0, 2)
    for number in range(1, SWEEPS_H + 1):
        heart.finish(number, number + 1, 1)
    for number in range(1, SWEEPS_T):
        torso.finish(number, number + 1, 1)

    def take_back(step, carry):
        other, _ = peer_at(step)
        landed(step, returned, came, back_sem, home_sem).wait_recv()
        row_hot, col_hot = spots(send_node, send_count, other, rows_h, hshape[2])
        return carry + place_at(came[other], row_hot, col_hot)

    row_hot, col_hot = spots(send_node, send_count, me, rows_h, hshape[2])
    flux = place_at(came[me], row_hot, col_hot)
    flux = lax.fori_loop(1, peers, take_back, flux, unroll=unroll)
    flux = (flux[:, : hshape[2]] + flux[:, hshape[2] :]).reshape(layer_h, hshape[1], hshape[2])
    heart_phi[0:layer_h] = phi_new[:layer_h] - flux * (
        inverse[:layer_h] * (1.0 / (intra_cond + extra_cond))
    )

    def settle(step, carry):
        landed(step, sent, arrived, out_sem, in_sem).wait_send()
        landed(step, returned, came, back_sem, home_sem).wait_send()
        return carry

    lax.fori_loop(1, peers, settle, 0, unroll=unroll)


def per_device(sizes, *args):
    (
        states,
        membrane,
        phi_heart,
        ion_params,
        torso_phi,
        tissue_scale,
        labels,
        cond_table,
        send_node,
        send_count,
        recv_voxel,
        recv_count,
    ) = args
    peers, cap = send_node.shape[-2:]
    hx, hy, hz = membrane.shape
    tx, ty, tz = torso_phi.shape
    vmem = pl.BlockSpec(memory_space=pltpu.VMEM)
    smem = pl.BlockSpec(memory_space=pltpu.SMEM)

    def grid_scratch(shape, slots, turns):
        nx, ny, nz = shape
        faces = [
            pltpu.VMEM((2, slots, ny, nz), F32),
            pltpu.VMEM((2, slots, nx, 1, nz), F32),
            pltpu.VMEM((2, slots, 1, nx * ny), F32),
        ]
        return (
            faces
            + faces
            + [
                pltpu.VMEM((nx, ny + 16, nz), F32),
                pltpu.SemaphoreType.DMA((turns, 3, 2)),
                pltpu.SemaphoreType.DMA((turns, 3, 2)),
            ]
        )

    patches = [pltpu.VMEM((peers, 1, cap), F32)] * 4
    signals = [pltpu.SemaphoreType.DMA((peers,))] * 4
    block = pltpu.VMEM((hx, hy, hz), F32)
    work = [
        block,
        block,
        block,
        pltpu.VMEM((6, tx, ty, tz), F32),
        pltpu.VMEM((tx, ty, tz), F32),
        pltpu.VMEM((tx // 4, ty, tz), F32),
        pltpu.VMEM((tx // 4 * ty, tz), F32),
        pltpu.VMEM((hx // 4 * hy, hz), F32),
    ]
    return pl.pallas_call(
        functools.partial(kernel, sizes),
        out_shape=(
            jax.ShapeDtypeStruct(membrane.shape, F32),
            jax.ShapeDtypeStruct(membrane.shape, F32),
            jax.ShapeDtypeStruct(torso_phi.shape, F32),
        ),
        in_specs=[vmem, vmem, vmem, smem, vmem, vmem, vmem, smem, vmem, smem, vmem, smem],
        out_specs=(vmem, vmem, vmem),
        scratch_shapes=grid_scratch(membrane.shape, SWEEPS_H + 2, SWEEPS_H + 1)
        + grid_scratch(torso_phi.shape, SWEEPS_T + 1, SWEEPS_T)
        + patches
        + signals
        + work,
        compiler_params=pltpu.CompilerParams(
            collective_id=0, has_side_effects=True, vmem_limit_bytes=48 * 1024 * 1024
        ),
    )(
        states,
        membrane,
        phi_heart,
        ion_params,
        torso_phi,
        tissue_scale,
        labels,
        cond_table,
        send_node.reshape(peers, cap),
        send_count.reshape(peers),
        recv_voxel.reshape(peers, cap),
        recv_count.reshape(peers),
    )


def solution(mesh):
    sizes = (mesh.shape["grp"], mesh.shape["gx"], mesh.shape["gy"])
    placed = (
        P(None, "gx", "gy", "grp"),
        P("gx", "gy", "grp"),
        P("gx", "gy", "grp"),
        P(),
        P("gx", "gy", "grp"),
        P("gx", "gy", "grp"),
        P("gx", "gy", "grp"),
        P(),
        P("grp", "gx", "gy", None, None),
        P("grp", "gx", "gy", None),
        P("grp", "gx", "gy", None, None),
        P("grp", "gx", "gy", None),
    )
    return jax.shard_map(
        functools.partial(per_device, sizes),
        mesh=mesh,
        in_specs=placed,
        out_specs=(P("gx", "gy", "grp"), P("gx", "gy", "grp"), P("gx", "gy", "grp")),
        check_vma=False,
    )
```

```python
import functools

import jax
import jax.numpy as jnp
from jax import lax
from jax.experimental import pallas as pl
from jax.experimental.pallas import tpu as pltpu
from jax.sharding import PartitionSpec as P

LABELS = 4
SWEEPS_H = 3
SWEEPS_T = 4

time_step = 0.1
intra_cond = 0.25
extra_cond = 0.5
penalty = 2.0
cheb_low = 0.1
cheb_high = 2.0

MESH = pl.DeviceIdType.MESH
F32 = jnp.float32
BF16 = jnp.bfloat16


def cheb_coeffs(sweeps):
    centre = 0.5 * (cheb_high + cheb_low)
    half_width = 0.5 * (cheb_high - cheb_low)
    scaled = centre / half_width
    coeffs = [(0.0, 1.0 / centre)]
    rho_old = 1.0 / scaled
    for number in range(1, sweeps):
        rho_new = 1.0 / (2.0 * scaled - rho_old)
        coeffs.append((rho_new * rho_old, 2.0 * rho_new / half_width))
        rho_old = rho_new
    return coeffs


def harmonic(a, b):
    return 2.0 * a * b / (a + b)


def two_terms(values):
    high = values.astype(BF16)
    return high, (values - high.astype(F32)).astype(BF16)


class Grid:
    def __init__(self, shape, stage, landing, sends, recvs, ypad, place):
        self.shape = shape
        self.stage = stage
        self.landing = landing
        self.sends = sends
        self.recvs = recvs
        self.ypad = ypad
        self.place = place

    def clear_ends(self):
        for axis, (_, low, high) in enumerate(self.place):
            for side, (_, present) in enumerate((low, high)):
                if present is None:
                    continue

                @pl.when(jnp.logical_not(present))
                def _(axis=axis, side=side):
                    ref = self.landing[axis]
                    ref[side] = jnp.zeros(ref.shape[1:], F32)

    def pack(self, slot, field):
        nx, ny, nz = self.shape
        xs, ys, zs = self.stage
        xs[0, slot] = field[0]
        xs[1, slot] = field[nx - 1]
        ys[0, slot] = field[:, 0:1, :]
        ys[1, slot] = field[:, ny - 1 : ny, :]
        turned = jnp.transpose(field.reshape(nx * ny, nz))
        zs[0, slot] = turned[0:1, :]
        zs[1, slot] = turned[nz - 1 : nz, :]

    def copies(self, turn, first, count):
        for axis, (name, low, high) in enumerate(self.place):
            for side, there in enumerate((low, high)):
                back = (high, low)[side]
                yield (
                    pltpu.make_async_remote_copy(
                        src_ref=self.stage[axis].at[side, pl.ds(first, count)],
                        dst_ref=self.landing[axis].at[1 - side, pl.ds(first, count)],
                        send_sem=self.sends.at[turn, axis, side],
                        recv_sem=self.recvs.at[turn, axis, 1 - side],
                        device_id={name: there[0]},
                        device_id_type=MESH,
                    ),
                    there[1],
                    back[1],
                )

    def send(self, turn, first, count):
        for copy, out, _ in self.copies(turn, first, count):
            if out is None:
                copy.start()
            else:
                pl.when(out)(copy.start)

    def wait(self, turn, first, count):
        for copy, _, back in self.copies(turn, first, count):
            if back is None:
                copy.wait_recv()
            else:
                pl.when(back)(copy.wait_recv)

    def finish(self, turn, first, count):
        for copy, out, _ in self.copies(turn, first, count):
            if out is None:
                copy.wait_send()
            else:
                pl.when(out)(copy.wait_send)

    def around(self, slot, field):
        nx, ny, nz = self.shape
        rx, ry, rz = self.landing
        below_x = jnp.concatenate([rx[0, slot][None], field[:-1]], axis=0)
        above_x = jnp.concatenate([field[1:], rx[1, slot][None]], axis=0)
        self.ypad[:, 8 : 8 + ny, :] = field
        self.ypad[:, 7:8, :] = ry[0, slot]
        self.ypad[:, 8 + ny : 9 + ny, :] = ry[1, slot]
        below_y = self.ypad[:, 7 : 7 + ny, :]
        above_y = self.ypad[:, 9 : 9 + ny, :]
        depth = lax.broadcasted_iota(jnp.int32, (nz, nx * ny), 0)
        ends = jnp.transpose(jnp.where(depth == 0, rz[0, slot], rz[1, slot]))
        flat = field.reshape(nx * ny, nz)
        lanes = lax.broadcasted_iota(jnp.int32, (nx * ny, nz), 1)
        below_z = jnp.where(lanes == 0, ends, pltpu.roll(flat, 1, 1)).reshape(nx, ny, nz)
        above_z = jnp.where(lanes == nz - 1, ends, pltpu.roll(flat, nz - 1, 1)).reshape(nx, ny, nz)
        return below_x, above_x, below_y, above_y, below_z, above_z


def turned_table(layer, rows, width):
    high, low = two_terms(jnp.transpose(layer.reshape(rows, width)))
    return jnp.concatenate([high, low], axis=1)


class Patch:
    def __init__(self, nodes, counts, row_hots, columns, rows, width):
        self.nodes = nodes
        self.counts = counts
        self.row_hots = row_hots
        self.columns = columns
        self.rows = rows
        self.width = width
        self.cap = nodes.shape[1]

    def prepare(self, peer):
        index = self.nodes[pl.ds(peer, 1), :]
        slot_ids = lax.broadcasted_iota(jnp.int32, (1, self.cap), 1)
        index = jnp.where(slot_ids < self.counts[peer], index, -1)
        row_ids = lax.broadcasted_iota(jnp.int32, (self.rows, self.cap), 0)
        row = lax.shift_right_arithmetic(index, self.width.bit_length() - 1)
        self.row_hots[peer] = jnp.where(row_ids == row, 1.0, 0.0).astype(BF16)
        self.columns[peer] = index & (self.width - 1)

    def column_mask(self, peer):
        col_ids = lax.broadcasted_iota(jnp.int32, (self.width, self.cap), 0)
        return col_ids == self.columns[peer]

    def pick(self, table, peer):
        row_hot = self.row_hots[peer]
        chosen = jnp.dot(
            table, jnp.concatenate([row_hot, row_hot], axis=0), preferred_element_type=F32
        )
        return jnp.sum(jnp.where(self.column_mask(peer), chosen, 0.0), axis=0, keepdims=True)

    def weigh(self, peer):
        ones = jnp.where(self.column_mask(peer), 1.0, 0.0).astype(BF16)
        return lax.dot_general(
            self.row_hots[peer], ones, (((1,), (1,)), ((), ())), preferred_element_type=F32
        )

    def place_at(self, values, peer):
        mask = self.column_mask(peer)
        high = values.astype(BF16).astype(F32)
        low = values - high
        spread = jnp.concatenate(
            [jnp.where(mask, high, 0.0).astype(BF16), jnp.where(mask, low, 0.0).astype(BF16)],
            axis=0,
        )
        return lax.dot_general(
            self.row_hots[peer], spread, (((1,), (1,)), ((), ())), preferred_element_type=F32
        )


def kernel(
    sizes,
    states_in,
    membrane_in,
    phi_heart_in,
    ion_params_in,
    torso_phi_in,
    tissue_scale_in,
    labels_in,
    cond_table_in,
    send_node_in,
    send_count_in,
    recv_voxel_in,
    recv_count_in,
    new_membrane_out,
    heart_phi_out,
    torso_out_out,
    new_membrane, heart_phi, torso_out, store_sem,
    states, membrane, phi_heart, ion_params, torso_phi, tissue_scale, labels, cond_table,
    send_node, send_count, recv_voxel, recv_count, load_sem,
    hsx, hsy, hsz, hrx, hry, hrz, hypad, hsend, hrecv,
    tsx, tsy, tsz, trx, try_, trz, typad, tsend, trecv,
    sent, arrived, returned, came,
    out_sem, in_sem, back_sem, home_sem,
    phi_h, source_h, current_h, gains, update_t, right_t, weight_t,
    rows_node, cols_node, rows_voxel, cols_voxel,
):
    n_grp, n_gx, n_gy = sizes
    peers = n_gx * n_gy
    group = 8 if peers % 8 == 0 else 1
    g = lax.axis_index("grp")
    i = lax.axis_index("gx")
    j = lax.axis_index("gy")
    me = i * n_gy + j
    hshape = membrane.shape
    tshape = torso_phi.shape

    sources = (
        (membrane_in, membrane), (phi_heart_in, phi_heart), (tissue_scale_in, tissue_scale),
        (labels_in, labels), (cond_table_in, cond_table), (torso_phi_in, torso_phi),
        (ion_params_in, ion_params), (states_in, states), (send_node_in, send_node),
        (send_count_in, send_count), (recv_voxel_in, recv_voxel), (recv_count_in, recv_count),
    )
    stores = [
        pltpu.make_async_copy(new_membrane, new_membrane_out, store_sem.at[0]),
        pltpu.make_async_copy(torso_out, torso_out_out, store_sem.at[1]),
        pltpu.make_async_copy(heart_phi, heart_phi_out, store_sem.at[2]),
    ]
    loads = [
        pltpu.make_async_copy(there, here, load_sem.at[number])
        for number, (there, here) in enumerate(sources)
    ]
    for load in loads:
        load.start()

    place = (
        ("gx", (lax.rem(i + n_gx - 1, n_gx), None), (lax.rem(i + 1, n_gx), None)),
        ("gy", (jnp.maximum(j - 1, 0), j > 0), (jnp.minimum(j + 1, n_gy - 1), j < n_gy - 1)),
        ("grp", (jnp.maximum(g - 1, 0), g > 0), (jnp.minimum(g + 1, n_grp - 1), g < n_grp - 1)),
    )
    heart = Grid(hshape, (hsx, hsy, hsz), (hrx, hry, hrz), hsend, hrecv, hypad, place)
    torso = Grid(tshape, (tsx, tsy, tsz), (trx, try_, trz), tsend, trecv, typad, place)
    heart.clear_ends()
    torso.clear_ends()

    def peer_at(step):
        other = lax.rem(me + step, peers)
        return other, {"gx": other // n_gy, "gy": lax.rem(other, n_gy)}

    barrier = pltpu.get_barrier_semaphore()

    def greet(step, carry):
        pl.semaphore_signal(barrier, inc=1, device_id=peer_at(step)[1], device_id_type=MESH)
        return carry

    lax.fori_loop(1, peers, greet, 0, unroll=peers <= 8)
    _, low_z, high_z = place[2]
    for there, present in (low_z, high_z):

        @pl.when(present)
        def _(there=there):
            pl.semaphore_signal(barrier, inc=1, device_id={"grp": there}, device_id_type=MESH)

    loads[0].wait()
    voltage = membrane[...]
    heart.pack(0, voltage)
    loads[1].wait()
    heart.pack(1, phi_heart[...])
    pl.semaphore_wait(
        barrier, peers - 1 + (g > 0).astype(jnp.int32) + (g < n_grp - 1).astype(jnp.int32)
    )
    heart.send(0, 0, 2)

    for load in loads[2:6]:
        load.wait()
    names = labels[...]
    table = jnp.where(names == 0, cond_table[0], 0.0)
    for number in range(1, LABELS):
        table = jnp.where(names == number, cond_table[number], table)
    conduct = tissue_scale[...] * table
    torso.pack(0, conduct)
    torso.pack(1, torso_phi[...])
    torso.send(0, 0, 2)

    loads[6].wait()
    loads[7].wait()
    current = jnp.zeros(hshape, F32)
    for state in range(states.shape[0]):
        line = jnp.zeros((1, 1, hshape[2]), F32)
        half_slope = 0.5 / (line + ion_params[1, state])
        decay = jnp.exp(line - time_step * ion_params[2, state])
        steady = 0.5 + 0.5 * jnp.tanh((voltage - ion_params[0, state]) * half_slope)
        gate = steady + (states[state].astype(F32) - steady) * decay
        current = current + ion_params[3, state] * gate * (voltage - ion_params[4, state])
    current_h[...] = current

    ny = lax.broadcasted_iota(jnp.int32, hshape, 1) + j * hshape[1]
    nz = lax.broadcasted_iota(jnp.int32, hshape, 2) + g * hshape[2]
    diag = (
        6.0
        - jnp.where(ny == 0, 1.0, 0.0)
        - jnp.where(ny == hshape[1] * n_gy - 1, 1.0, 0.0)
        - jnp.where(nz == 0, 1.0, 0.0)
        - jnp.where(nz == hshape[2] * n_grp - 1, 1.0, 0.0)
    )
    inverse = 1.0 / diag

    def total_of(parts):
        return ((parts[0] + parts[1]) + (parts[2] + parts[3])) + (parts[4] + parts[5])

    layer_h = hshape[0] // 4
    rows_h = layer_h * hshape[1]
    layer = tshape[0] // 4
    rows = layer * tshape[1]
    width = tshape[2]
    nodes = Patch(send_node, send_count, rows_node, cols_node, rows_h, hshape[2])
    voxels = Patch(recv_voxel, recv_count, rows_voxel, cols_voxel, rows, width)

    def over_peers(body, start):
        def one_group(number, carry):
            for offset in range(group):
                carry = body(number * group + offset, carry)
            return carry

        if peers == group:
            return one_group(0, start)
        return lax.fori_loop(0, peers // group, one_group, start)

    def indices():
        for load in loads[8:]:
            load.wait()

        def prepare(peer, carry):
            nodes.prepare(peer)
            voxels.prepare(peer)
            return carry + voxels.weigh(peer)

        weight_t[...] = penalty * over_peers(prepare, jnp.zeros((rows, width), F32))

    def conductances():
        torso.wait(0, 0, 2)
        faces = [harmonic(conduct, other) for other in torso.around(0, conduct)]
        weight = weight_t[...].reshape(layer, tshape[1], width)
        total = total_of(faces)
        total = jnp.concatenate([total[:layer] + weight, total[layer:]], axis=0)
        scale = 1.0 / total
        for number in range(6):
            gains[number] = faces[number] * scale
        right_t[...] = penalty * scale[:layer]

    def torso_residue(slot, field):
        return -field + total_of(
            [gains[n] * other for n, other in enumerate(torso.around(slot, field))]
        )

    heart.wait(0, 0, 2)
    lap_mem = diag * voltage - total_of(heart.around(0, voltage))
    source_h[...] = lap_mem
    base = (-intra_cond / (intra_cond + extra_cond)) * lap_mem * inverse
    iterate = phi_heart[...]
    update = None
    for number, (carry_coef, resid_coef) in enumerate(cheb_coeffs(SWEEPS_H)):
        if number > 0:
            heart.wait(number, number + 1, 1)
        around = total_of(heart.around(number + 1, iterate))
        residue = base - iterate + around * inverse
        update = resid_coef * residue if update is None else carry_coef * update + resid_coef * residue
        iterate = iterate + update
        if number < SWEEPS_H - 1:
            heart.pack(number + 2, iterate)
            heart.send(number + 1, number + 2, 1)
        if number == 0:
            indices()
        if number == 1:
            conductances()
    phi_new = iterate
    phi_h[...] = phi_new

    def patch(other, source, target, sends, recvs, mine):
        return pltpu.make_async_remote_copy(
            src_ref=source.at[other],
            dst_ref=target.at[mine],
            send_sem=sends.at[other],
            recv_sem=recvs.at[mine],
            device_id={"gx": other // n_gy, "gy": lax.rem(other, n_gy)},
            device_id_type=MESH,
        )

    to_torso = (sent, arrived, out_sem, in_sem)
    to_heart = (returned, came, back_sem, home_sem)

    def post(buffers, fill):
        source, target = buffers[:2]

        def one_group(number, carry):
            picked = [fill(number * group + offset) for offset in range(group)]
            for offset in range(group):
                source[number * group + offset] = picked[offset]
            return carry

        if peers == group:
            one_group(0, 0)
        else:
            lax.fori_loop(0, peers // group, one_group, 0)

        def start(step, carry):
            patch(peer_at(step)[0], *buffers, me).start()
            return carry

        lax.fori_loop(1, peers, start, 0, unroll=peers <= 8)
        target[me] = source[me]

    def receive(buffers):
        def land(step, carry):
            other = peer_at(step)[0]
            patch(other, *buffers, other).wait_recv()
            return carry

        lax.fori_loop(1, peers, land, 0, unroll=peers <= 8)

    table_h = turned_table(phi_new[:layer_h], rows_h, hshape[2])
    post(to_torso, lambda peer: nodes.pick(table_h, peer))
    heart.pack(SWEEPS_H + 1, phi_new)
    heart.send(SWEEPS_H, SWEEPS_H + 1, 1)

    iterate = torso_phi[...]
    update_t[...] = torso_residue(1, iterate)

    receive(to_torso)
    summed = over_peers(
        lambda peer, carry: carry + voxels.place_at(arrived[peer], peer),
        jnp.zeros((rows, 2 * width), F32),
    )
    summed = summed[:, :width] + summed[:, width:]
    right = summed.reshape(layer, tshape[1], width) * right_t[...]
    right_t[...] = right

    coeffs = cheb_coeffs(SWEEPS_T)
    update = update_t[...]
    update = coeffs[0][1] * jnp.concatenate([update[:layer] + right, update[layer:]], axis=0)
    iterate = iterate + update
    for number in range(1, SWEEPS_T):
        torso.pack(number + 1, iterate)
        torso.send(number, number + 1, 1)
        if number == 1:
            phi_new = phi_h[...]
            heart.wait(SWEEPS_H, SWEEPS_H + 1, 1)
            lap_phi = diag * phi_new - total_of(heart.around(SWEEPS_H + 1, phi_new))
            new_membrane[...] = membrane[...] + time_step * (
                -intra_cond * (source_h[...] + lap_phi) - current_h[...]
            )
            stores[0].start()
        torso.wait(number, number + 1, 1)
        residue = torso_residue(number + 1, iterate)
        residue = jnp.concatenate([residue[:layer] + right_t[...], residue[layer:]], axis=0)
        update = coeffs[number][0] * update + coeffs[number][1] * residue
        iterate = iterate + update
    table_t = turned_table(iterate[:layer], rows, width)
    post(
        to_heart, lambda peer: penalty * (arrived[peer] - voxels.pick(table_t, peer))
    )
    torso_out[...] = iterate
    stores[1].start()
    phi_new = phi_h[...]
    heart_phi[...] = phi_new

    heart.finish(0, 0, 2)
    torso.finish(0, 0, 2)
    for number in range(1, SWEEPS_H + 1):
        heart.finish(number, number + 1, 1)
    for number in range(1, SWEEPS_T):
        torso.finish(number, number + 1, 1)

    receive(to_heart)
    flux = over_peers(
        lambda peer, carry: carry + nodes.place_at(came[peer], peer),
        jnp.zeros((rows_h, 2 * hshape[2]), F32),
    )
    flux = (flux[:, : hshape[2]] + flux[:, hshape[2] :]).reshape(layer_h, hshape[1], hshape[2])
    heart_phi[0:layer_h] = phi_new[:layer_h] - flux * (
        inverse[:layer_h] * (1.0 / (intra_cond + extra_cond))
    )
    stores[2].start()

    def settle(step, carry):
        other = peer_at(step)[0]
        patch(other, *to_torso, other).wait_send()
        patch(other, *to_heart, other).wait_send()
        return carry

    lax.fori_loop(1, peers, settle, 0, unroll=peers <= 8)
    for store in stores:
        store.wait()


def write_out(first, second, third, first_out, second_out, third_out, sems):
    copies = [
        pltpu.make_async_copy(here, there, sems.at[number])
        for number, (here, there) in enumerate(
            ((first, first_out), (second, second_out), (third, third_out))
        )
    ]
    for copy in copies:
        copy.start()
    for copy in copies:
        copy.wait()


def per_device(sizes, *args):
    peers, cap = args[8].shape[-2:]
    args = list(args)
    for number in (8, 10):
        args[number] = args[number].reshape(peers, cap)
    for number in (9, 11):
        args[number] = args[number].reshape(peers)
    hshape = args[1].shape
    tshape = args[4].shape
    hx, hy, hz = hshape
    tx, ty, tz = tshape
    hbm = pl.BlockSpec(memory_space=pltpu.HBM)
    in_smem = (3, 7, 9, 11)

    def grid_scratch(shape, slots, turns):
        nx, ny, nz = shape
        faces = [
            pltpu.VMEM((2, slots, ny, nz), F32),
            pltpu.VMEM((2, slots, nx, 1, nz), F32),
            pltpu.VMEM((2, slots, 1, nx * ny), F32),
        ]
        return (
            faces
            + faces
            + [
                pltpu.VMEM((nx, ny + 16, nz), F32),
                pltpu.SemaphoreType.DMA((turns, 3, 2)),
                pltpu.SemaphoreType.DMA((turns, 3, 2)),
            ]
        )

    staged = [
        pltpu.VMEM(hshape, F32),
        pltpu.VMEM(hshape, F32),
        pltpu.VMEM(tshape, F32),
        pltpu.SemaphoreType.DMA((3,)),
    ] + [
        (pltpu.SMEM if number in in_smem else pltpu.VMEM)(array.shape, array.dtype)
        for number, array in enumerate(args)
    ] + [pltpu.SemaphoreType.DMA((len(args),))]
    patches = [pltpu.VMEM((peers, 1, cap), F32)] * 4
    signals = [pltpu.SemaphoreType.DMA((peers,))] * 4
    rows_h = hx // 4 * hy
    rows = tx // 4 * ty
    work = [
        pltpu.VMEM(hshape, F32),
        pltpu.VMEM(hshape, F32),
        pltpu.VMEM(hshape, F32),
        pltpu.VMEM((6, tx, ty, tz), F32),
        pltpu.VMEM(tshape, F32),
        pltpu.VMEM((tx // 4, ty, tz), F32),
        pltpu.VMEM((rows, tz), F32),
        pltpu.VMEM((peers, rows_h, cap), BF16),
        pltpu.VMEM((peers, 1, cap), jnp.int32),
        pltpu.VMEM((peers, rows, cap), BF16),
        pltpu.VMEM((peers, 1, cap), jnp.int32),
    ]
    shapes = tuple(jax.ShapeDtypeStruct(shape, F32) for shape in (hshape, hshape, tshape))
    results = pl.pallas_call(
        functools.partial(kernel, sizes),
        out_shape=shapes,
        in_specs=[hbm] * len(args),
        out_specs=(hbm, hbm, hbm),
        scratch_shapes=staged
        + grid_scratch(hshape, SWEEPS_H + 2, SWEEPS_H + 1)
        + grid_scratch(tshape, SWEEPS_T + 1, SWEEPS_T)
        + patches
        + signals
        + work,
        compiler_params=pltpu.CompilerParams(
            collective_id=0, has_side_effects=True, vmem_limit_bytes=64 * 1024 * 1024
        ),
    )(*args)
    return pl.pallas_call(
        write_out,
        out_shape=shapes,
        in_specs=[hbm, hbm, hbm],
        out_specs=(hbm, hbm, hbm),
        scratch_shapes=[pltpu.SemaphoreType.DMA((3,))],
        compiler_params=pltpu.CompilerParams(vmem_limit_bytes=64 * 1024 * 1024),
    )(*results)


def solution(mesh):
    sizes = (mesh.shape["grp"], mesh.shape["gx"], mesh.shape["gy"])
    placed = (
        P(None, "gx", "gy", "grp"),
        P("gx", "gy", "grp"),
        P("gx", "gy", "grp"),
        P(),
        P("gx", "gy", "grp"),
        P("gx", "gy", "grp"),
        P("gx", "gy", "grp"),
        P(),
        P("grp", "gx", "gy", None, None),
        P("grp", "gx", "gy", None),
        P("grp", "gx", "gy", None, None),
        P("grp", "gx", "gy", None),
    )
    return jax.shard_map(
        functools.partial(per_device, sizes),
        mesh=mesh,
        in_specs=placed,
        out_specs=(P("gx", "gy", "grp"), P("gx", "gy", "grp"), P("gx", "gy", "grp")),
        check_vma=False,
    )
```

```python
import functools

import jax
import jax.numpy as jnp
from jax import lax
from jax.experimental import pallas as pl
from jax.experimental.pallas import tpu as pltpu
from jax.sharding import PartitionSpec as P

LABELS = 4
SWEEPS_H = 3
SWEEPS_T = 4

time_step = 0.1
intra_cond = 0.25
extra_cond = 0.5
penalty = 2.0
cheb_low = 0.1
cheb_high = 2.0

MESH = pl.DeviceIdType.MESH
F32 = jnp.float32
BF16 = jnp.bfloat16


def cheb_coeffs(sweeps):
    centre = 0.5 * (cheb_high + cheb_low)
    half_width = 0.5 * (cheb_high - cheb_low)
    scaled = centre / half_width
    coeffs = [(0.0, 1.0 / centre)]
    rho_old = 1.0 / scaled
    for number in range(1, sweeps):
        rho_new = 1.0 / (2.0 * scaled - rho_old)
        coeffs.append((rho_new * rho_old, 2.0 * rho_new / half_width))
        rho_old = rho_new
    return coeffs


def harmonic(a, b):
    return 2.0 * a * b / (a + b)


def two_terms(values):
    high = values.astype(BF16)
    return high, (values - high.astype(F32)).astype(BF16)


class Grid:
    def __init__(self, shape, stage, landing, sends, recvs, ypad, place, partial):
        self.shape = shape
        self.stage = stage
        self.landing = landing
        self.sends = sends
        self.recvs = recvs
        self.ypad = ypad
        self.partial = partial
        self.place = place

    def clear_ends(self):
        nx, ny, nz = self.shape
        self.ypad[:, 7:8, :] = jnp.zeros((nx, 1, nz), F32)
        self.ypad[:, 8 + ny : 9 + ny, :] = jnp.zeros((nx, 1, nz), F32)
        for axis, (_, low, high) in enumerate(self.place):
            for side, (_, present) in enumerate((low, high)):
                if present is None:
                    continue

                @pl.when(jnp.logical_not(present))
                def _(axis=axis, side=side):
                    ref = self.landing[axis]
                    ref[side] = jnp.zeros(ref.shape[1:], F32)

    def pack(self, slot, field):
        nx, ny, nz = self.shape
        xs, ys, zs = self.stage
        xs[0, slot] = field[0]
        xs[1, slot] = field[nx - 1]
        ys[0, slot] = field[:, 0:1, :]
        ys[1, slot] = field[:, ny - 1 : ny, :]
        turned = jnp.transpose(field.reshape(nx * ny, nz))
        zs[0, slot] = turned[0:1, :]
        zs[1, slot] = turned[nz - 1 : nz, :]

    def copies(self, turn, first, count):
        for axis, (name, low, high) in enumerate(self.place):
            for side, there in enumerate((low, high)):
                back = (high, low)[side]
                yield (
                    pltpu.make_async_remote_copy(
                        src_ref=self.stage[axis].at[side, pl.ds(first, count)],
                        dst_ref=self.landing[axis].at[1 - side, pl.ds(first, count)],
                        send_sem=self.sends.at[turn, axis, side],
                        recv_sem=self.recvs.at[turn, axis, 1 - side],
                        device_id={name: there[0]},
                        device_id_type=MESH,
                    ),
                    there[1],
                    back[1],
                )

    def send(self, turn, first, count):
        for copy, out, _ in self.copies(turn, first, count):
            if out is None:
                copy.start()
            else:
                pl.when(out)(copy.start)

    def wait(self, turn, first, count):
        for copy, _, back in self.copies(turn, first, count):
            if back is None:
                copy.wait_recv()
            else:
                pl.when(back)(copy.wait_recv)

    def finish(self, turn, first, count):
        for copy, out, _ in self.copies(turn, first, count):
            if out is None:
                copy.wait_send()
            else:
                pl.when(out)(copy.wait_send)

    def inside(self, field):
        nx, ny, nz = self.shape
        none = jnp.zeros((1, ny, nz), F32)
        below_x = jnp.concatenate([none, field[:-1]], axis=0)
        above_x = jnp.concatenate([field[1:], none], axis=0)
        self.ypad[:, 8 : 8 + ny, :] = field
        below_y = self.ypad[:, 7 : 7 + ny, :]
        above_y = self.ypad[:, 9 : 9 + ny, :]
        flat = field.reshape(nx * ny, nz)
        lanes = lax.broadcasted_iota(jnp.int32, (nx * ny, nz), 1)
        below_z = jnp.where(lanes == 0, 0.0, pltpu.roll(flat, 1, 1)).reshape(nx, ny, nz)
        above_z = jnp.where(lanes == nz - 1, 0.0, pltpu.roll(flat, nz - 1, 1)).reshape(nx, ny, nz)
        return below_x, above_x, below_y, above_y, below_z, above_z

    def begin(self, field, gains=None, which=0):
        parts = self.inside(field)
        if gains is not None:
            parts = [gains[number] * part for number, part in enumerate(parts)]
        self.partial[which] = total_of(parts)

    def ends(self, slot):
        nx, ny, nz = self.shape
        rz = self.landing[2]
        depth = lax.broadcasted_iota(jnp.int32, (nz, nx * ny), 0)
        turned = jnp.where(depth == 0, rz[0, slot], jnp.where(depth == nz - 1, rz[1, slot], 0.0))
        return jnp.transpose(turned).reshape(nx, ny, nz)

    def complete(self, slot, gains=None, end_gain=None, which=0):
        nx, ny, nz = self.shape
        rx, ry, _ = self.landing
        ends = self.ends(slot)
        for side, at in ((0, 0), (1, nx - 1)):
            other = rx[side, slot]
            if gains is not None:
                other = gains[side, at] * other
            self.partial[which, at] = self.partial[which, at] + other
        for side, at in ((0, 0), (1, ny - 1)):
            other = ry[side, slot]
            if gains is not None:
                other = gains[2 + side, :, at : at + 1, :] * other
            self.partial[which, :, at : at + 1, :] = self.partial[which, :, at : at + 1, :] + other
        if end_gain is not None:
            ends = end_gain[...] * ends
        return self.partial[which] + ends

    def around(self, slot, field):
        nx, ny, nz = self.shape
        rx, ry, _ = self.landing
        below_x, above_x, below_y, above_y, below_z, above_z = self.inside(field)
        below_x = jnp.concatenate([rx[0, slot][None], below_x[1:]], axis=0)
        above_x = jnp.concatenate([above_x[:-1], rx[1, slot][None]], axis=0)
        rows = lax.broadcasted_iota(jnp.int32, (nx, ny, nz), 1)
        below_y = jnp.where(rows == 0, ry[0, slot], below_y)
        above_y = jnp.where(rows == ny - 1, ry[1, slot], above_y)
        lanes = lax.broadcasted_iota(jnp.int32, (nx, ny, nz), 2)
        ends = self.ends(slot)
        below_z = jnp.where(lanes == 0, ends, below_z)
        above_z = jnp.where(lanes == nz - 1, ends, above_z)
        return below_x, above_x, below_y, above_y, below_z, above_z


def total_of(parts):
    return ((parts[0] + parts[1]) + (parts[2] + parts[3])) + (parts[4] + parts[5])


def turned_table(layer, rows, width):
    high, low = two_terms(jnp.transpose(layer.reshape(rows, width)))
    return jnp.concatenate([high, low], axis=1)


class Patch:
    def __init__(self, nodes, counts, row_hots, columns, rows, width):
        self.nodes = nodes
        self.counts = counts
        self.row_hots = row_hots
        self.columns = columns
        self.rows = rows
        self.width = width
        self.cap = nodes.shape[1]

    def prepare(self, peer):
        index = self.nodes[pl.ds(peer, 1), :]
        slot_ids = lax.broadcasted_iota(jnp.int32, (1, self.cap), 1)
        index = jnp.where(slot_ids < self.counts[peer], index, -1)
        row_ids = lax.broadcasted_iota(jnp.int32, (self.rows, self.cap), 0)
        row = lax.shift_right_arithmetic(index, self.width.bit_length() - 1)
        self.row_hots[peer] = jnp.where(row_ids == row, 1.0, 0.0).astype(BF16)
        self.columns[peer] = index & (self.width - 1)

    def column_mask(self, peer):
        col_ids = lax.broadcasted_iota(jnp.int32, (self.width, self.cap), 0)
        return col_ids == self.columns[peer]

    def pick(self, table, peer):
        row_hot = self.row_hots[peer]
        chosen = jnp.dot(
            table, jnp.concatenate([row_hot, row_hot], axis=0), preferred_element_type=F32
        )
        return jnp.sum(jnp.where(self.column_mask(peer), chosen, 0.0), axis=0, keepdims=True)

    def weigh(self, peer):
        ones = jnp.where(self.column_mask(peer), 1.0, 0.0).astype(BF16)
        return lax.dot_general(
            self.row_hots[peer], ones, (((1,), (1,)), ((), ())), preferred_element_type=F32
        )

    def place_at(self, values, peer):
        mask = self.column_mask(peer)
        high = values.astype(BF16).astype(F32)
        low = values - high
        spread = jnp.concatenate(
            [jnp.where(mask, high, 0.0).astype(BF16), jnp.where(mask, low, 0.0).astype(BF16)],
            axis=0,
        )
        return lax.dot_general(
            self.row_hots[peer], spread, (((1,), (1,)), ((), ())), preferred_element_type=F32
        )


def kernel(
    sizes,
    states_in,
    membrane_in,
    phi_heart_in,
    ion_params_in,
    torso_phi_in,
    tissue_scale_in,
    labels_in,
    cond_table_in,
    send_node_in,
    send_count_in,
    recv_voxel_in,
    recv_count_in,
    new_membrane_out,
    heart_phi_out,
    torso_out_out,
    new_membrane, heart_phi, torso_out, store_sem,
    states, membrane, phi_heart, ion_params, torso_phi, tissue_scale, labels, cond_table,
    send_node, send_count, recv_voxel, recv_count, load_sem,
    hsx, hsy, hsz, hrx, hry, hrz, hypad, hsend, hrecv,
    tsx, tsy, tsz, trx, try_, trz, typad, tsend, trecv,
    sent, arrived, returned, came,
    out_sem, in_sem, back_sem, home_sem,
    hpart, tpart, end_gain, phi_h, source_h, current_h, gains, right_t, weight_t,
    rows_node, cols_node, rows_voxel, cols_voxel,
):
    n_grp, n_gx, n_gy = sizes
    peers = n_gx * n_gy
    group = 8 if peers % 8 == 0 else 1
    g = lax.axis_index("grp")
    i = lax.axis_index("gx")
    j = lax.axis_index("gy")
    me = i * n_gy + j
    hshape = membrane.shape
    tshape = torso_phi.shape

    sources = (
        (membrane_in, membrane), (phi_heart_in, phi_heart), (tissue_scale_in, tissue_scale),
        (labels_in, labels), (cond_table_in, cond_table), (torso_phi_in, torso_phi),
        (ion_params_in, ion_params), (states_in, states), (send_node_in, send_node),
        (send_count_in, send_count), (recv_voxel_in, recv_voxel), (recv_count_in, recv_count),
    )
    layer_h = hshape[0] // 4
    surface = pl.ds(0, layer_h)
    deep = pl.ds(layer_h, hshape[0] - layer_h)
    stores = [
        pltpu.make_async_copy(new_membrane, new_membrane_out, store_sem.at[0]),
        pltpu.make_async_copy(torso_out, torso_out_out, store_sem.at[1]),
        pltpu.make_async_copy(heart_phi.at[deep], heart_phi_out.at[deep], store_sem.at[2]),
        pltpu.make_async_copy(heart_phi.at[surface], heart_phi_out.at[surface], store_sem.at[3]),
    ]
    loads = [
        pltpu.make_async_copy(there, here, load_sem.at[number])
        for number, (there, here) in enumerate(sources)
    ]
    for load in loads:
        load.start()

    place = (
        ("gx", (lax.rem(i + n_gx - 1, n_gx), None), (lax.rem(i + 1, n_gx), None)),
        ("gy", (jnp.maximum(j - 1, 0), j > 0), (jnp.minimum(j + 1, n_gy - 1), j < n_gy - 1)),
        ("grp", (jnp.maximum(g - 1, 0), g > 0), (jnp.minimum(g + 1, n_grp - 1), g < n_grp - 1)),
    )
    heart = Grid(hshape, (hsx, hsy, hsz), (hrx, hry, hrz), hsend, hrecv, hypad, place, hpart)
    torso = Grid(tshape, (tsx, tsy, tsz), (trx, try_, trz), tsend, trecv, typad, place, tpart)
    heart.clear_ends()
    torso.clear_ends()

    def peer_at(step):
        other = lax.rem(me + step, peers)
        return other, {"gx": other // n_gy, "gy": lax.rem(other, n_gy)}

    barrier = pltpu.get_barrier_semaphore()

    def greet(step, carry):
        pl.semaphore_signal(barrier, inc=1, device_id=peer_at(step)[1], device_id_type=MESH)
        return carry

    lax.fori_loop(1, peers, greet, 0, unroll=peers <= 8)
    _, low_z, high_z = place[2]
    for there, present in (low_z, high_z):

        @pl.when(present)
        def _(there=there):
            pl.semaphore_signal(barrier, inc=1, device_id={"grp": there}, device_id_type=MESH)

    loads[0].wait()
    voltage = membrane[...]
    heart.pack(0, voltage)
    loads[1].wait()
    heart.pack(1, phi_heart[...])
    pl.semaphore_wait(
        barrier, peers - 1 + (g > 0).astype(jnp.int32) + (g < n_grp - 1).astype(jnp.int32)
    )
    heart.send(0, 0, 2)

    for load in loads[2:6]:
        load.wait()
    names = labels[...]
    table = jnp.where(names == 0, cond_table[0], 0.0)
    for number in range(1, LABELS):
        table = jnp.where(names == number, cond_table[number], table)
    conduct = tissue_scale[...] * table
    torso.pack(0, conduct)
    torso.pack(1, torso_phi[...])
    torso.send(0, 0, 2)

    def ionic(first, last):
        voltage = membrane[...]
        current = jnp.zeros(hshape, F32) if first == 0 else current_h[...]
        for state in range(first, last):
            line = jnp.zeros((1, 1, hshape[2]), F32)
            half_slope = 0.5 / (line + ion_params[1, state])
            decay = jnp.exp(line - time_step * ion_params[2, state])
            steady = 0.5 + 0.5 * jnp.tanh((voltage - ion_params[0, state]) * half_slope)
            gate = steady + (states[state].astype(F32) - steady) * decay
            current = current + ion_params[3, state] * gate * (voltage - ion_params[4, state])
        current_h[...] = current

    heart.begin(voltage, which=0)
    heart.begin(phi_heart[...], which=1)

    ny = lax.broadcasted_iota(jnp.int32, hshape, 1) + j * hshape[1]
    nz = lax.broadcasted_iota(jnp.int32, hshape, 2) + g * hshape[2]
    diag = (
        6.0
        - jnp.where(ny == 0, 1.0, 0.0)
        - jnp.where(ny == hshape[1] * n_gy - 1, 1.0, 0.0)
        - jnp.where(nz == 0, 1.0, 0.0)
        - jnp.where(nz == hshape[2] * n_grp - 1, 1.0, 0.0)
    )
    inverse = 1.0 / diag

    rows_h = layer_h * hshape[1]
    layer = tshape[0] // 4
    rows = layer * tshape[1]
    width = tshape[2]
    nodes = Patch(send_node, send_count, rows_node, cols_node, rows_h, hshape[2])
    voxels = Patch(recv_voxel, recv_count, rows_voxel, cols_voxel, rows, width)

    def over_peers(body, start):
        def one_group(number, carry):
            for offset in range(group):
                carry = body(number * group + offset, carry)
            return carry

        if peers == group:
            return one_group(0, start)
        return lax.fori_loop(0, peers // group, one_group, start)

    def indices():
        for load in loads[8:]:
            load.wait()

        def prepare(peer, carry):
            nodes.prepare(peer)
            voxels.prepare(peer)
            return carry + voxels.weigh(peer)

        weight_t[...] = penalty * over_peers(prepare, jnp.zeros((rows, width), F32))

    def conductances():
        torso.wait(0, 0, 2)
        faces = [harmonic(conduct, other) for other in torso.around(0, conduct)]
        weight = weight_t[...].reshape(layer, tshape[1], width)
        total = total_of(faces)
        total = jnp.concatenate([total[:layer] + weight, total[layer:]], axis=0)
        scale = 1.0 / total
        for number in range(6):
            gains[number] = faces[number] * scale
        lanes = lax.broadcasted_iota(jnp.int32, tshape, 2)
        end_gain[...] = jnp.where(
            lanes == 0, faces[4] * scale, jnp.where(lanes == width - 1, faces[5] * scale, 0.0)
        )
        right_t[...] = penalty * scale[:layer]

    indices()
    heart.wait(0, 0, 2)
    lap_mem = diag * voltage - heart.complete(0, which=0)
    source_h[...] = lap_mem
    base = (-intra_cond / (intra_cond + extra_cond)) * lap_mem * inverse
    iterate = phi_heart[...]
    update = None
    for number, (carry_coef, resid_coef) in enumerate(cheb_coeffs(SWEEPS_H)):
        if number > 0:
            heart.wait(number, number + 1, 1)
        around = heart.complete(number + 1, which=1)
        residue = base - iterate + around * inverse
        update = resid_coef * residue if update is None else carry_coef * update + resid_coef * residue
        iterate = iterate + update
        if number < SWEEPS_H - 1:
            heart.pack(number + 2, iterate)
            heart.send(number + 1, number + 2, 1)
            heart.begin(iterate, which=1)
        if number == 0:
            conductances()
        if number == 1:
            torso.begin(torso_phi[...], gains)
            partial = torso.complete(1, gains, end_gain)
            tpart[0] = partial
    phi_new = iterate
    phi_h[...] = phi_new

    def patch(other, source, target, sends, recvs, mine):
        return pltpu.make_async_remote_copy(
            src_ref=source.at[other],
            dst_ref=target.at[mine],
            send_sem=sends.at[other],
            recv_sem=recvs.at[mine],
            device_id={"gx": other // n_gy, "gy": lax.rem(other, n_gy)},
            device_id_type=MESH,
        )

    to_torso = (sent, arrived, out_sem, in_sem)
    to_heart = (returned, came, back_sem, home_sem)

    def post(buffers, fill):
        source, target = buffers[:2]

        def one_group(number, carry):
            picked = [fill(number * group + offset) for offset in range(group)]
            for offset in range(group):
                source[number * group + offset] = picked[offset]
            return carry

        if peers == group:
            one_group(0, 0)
        else:
            lax.fori_loop(0, peers // group, one_group, 0)

        def start(step, carry):
            patch(peer_at(step)[0], *buffers, me).start()
            return carry

        lax.fori_loop(1, peers, start, 0, unroll=peers <= 8)
        target[me] = source[me]

    def receive(buffers):
        def land(step, carry):
            other = peer_at(step)[0]
            patch(other, *buffers, other).wait_recv()
            return carry

        lax.fori_loop(1, peers, land, 0, unroll=peers <= 8)

    table_h = turned_table(phi_new[:layer_h], rows_h, hshape[2])
    post(to_torso, lambda peer: nodes.pick(table_h, peer))
    heart.pack(SWEEPS_H + 1, phi_new)
    heart.send(SWEEPS_H, SWEEPS_H + 1, 1)

    heart.begin(phi_new, which=1)
    half = states.shape[0] // 2
    loads[6].wait()
    loads[7].wait()
    ionic(0, half)
    receive(to_torso)
    summed = over_peers(
        lambda peer, carry: carry + voxels.place_at(arrived[peer], peer),
        jnp.zeros((rows, 2 * width), F32),
    )
    summed = summed[:, :width] + summed[:, width:]
    right = summed.reshape(layer, tshape[1], width) * right_t[...]
    right_t[...] = right

    coeffs = cheb_coeffs(SWEEPS_T)
    iterate = torso_phi[...]
    update = tpart[0] - iterate
    update = coeffs[0][1] * jnp.concatenate([update[:layer] + right, update[layer:]], axis=0)
    iterate = iterate + update
    for number in range(1, SWEEPS_T):
        torso.pack(number + 1, iterate)
        torso.send(number, number + 1, 1)
        torso.begin(iterate, gains)
        if number == 1:
            ionic(half, states.shape[0])
        if number == 2:
            phi_new = phi_h[...]
            heart.wait(SWEEPS_H, SWEEPS_H + 1, 1)
            lap_phi = diag * phi_new - heart.complete(SWEEPS_H + 1, which=1)
            new_membrane[...] = membrane[...] + time_step * (
                -intra_cond * (source_h[...] + lap_phi) - current_h[...]
            )
            stores[0].start()
        if number == SWEEPS_T - 1:
            heart_phi[layer_h:] = phi_h[layer_h:]
            stores[2].start()
        torso.wait(number, number + 1, 1)
        residue = torso.complete(number + 1, gains, end_gain) - iterate
        residue = jnp.concatenate([residue[:layer] + right_t[...], residue[layer:]], axis=0)
        update = coeffs[number][0] * update + coeffs[number][1] * residue
        iterate = iterate + update
    table_t = turned_table(iterate[:layer], rows, width)
    post(
        to_heart, lambda peer: penalty * (arrived[peer] - voxels.pick(table_t, peer))
    )
    torso_out[...] = iterate
    stores[1].start()
    phi_new = phi_h[...]

    heart.finish(0, 0, 2)
    torso.finish(0, 0, 2)
    for number in range(1, SWEEPS_H + 1):
        heart.finish(number, number + 1, 1)
    for number in range(1, SWEEPS_T):
        torso.finish(number, number + 1, 1)

    receive(to_heart)
    flux = over_peers(
        lambda peer, carry: carry + nodes.place_at(came[peer], peer),
        jnp.zeros((rows_h, 2 * hshape[2]), F32),
    )
    flux = (flux[:, : hshape[2]] + flux[:, hshape[2] :]).reshape(layer_h, hshape[1], hshape[2])
    heart_phi[0:layer_h] = phi_new[:layer_h] - flux * (
        inverse[:layer_h] * (1.0 / (intra_cond + extra_cond))
    )
    stores[3].start()

    def settle(step, carry):
        other = peer_at(step)[0]
        patch(other, *to_torso, other).wait_send()
        patch(other, *to_heart, other).wait_send()
        return carry

    lax.fori_loop(1, peers, settle, 0, unroll=peers <= 8)
    for store in stores:
        store.wait()


def write_out(*refs):
    sources, targets, held, (sems,) = refs[:3], refs[3:6], refs[6:9], refs[9:]
    ins = [
        pltpu.make_async_copy(there, here, sems.at[0, number])
        for number, (there, here) in enumerate(zip(sources, held))
    ]
    outs = [
        pltpu.make_async_copy(here, there, sems.at[1, number])
        for number, (here, there) in enumerate(zip(held, targets))
    ]
    for copy in ins:
        copy.start()
    for copy, after in zip(ins, outs):
        copy.wait()
        after.start()
    for copy in outs:
        copy.wait()


def per_device(sizes, *args):
    peers, cap = args[8].shape[-2:]
    args = list(args)
    for number in (8, 10):
        args[number] = args[number].reshape(peers, cap)
    for number in (9, 11):
        args[number] = args[number].reshape(peers)
    hshape = args[1].shape
    tshape = args[4].shape
    hx, hy, hz = hshape
    tx, ty, tz = tshape
    hbm = pl.BlockSpec(memory_space=pltpu.HBM)
    in_smem = (3, 7, 9, 11)

    def grid_scratch(shape, slots, turns):
        nx, ny, nz = shape
        faces = [
            pltpu.VMEM((2, slots, ny, nz), F32),
            pltpu.VMEM((2, slots, nx, 1, nz), F32),
            pltpu.VMEM((2, slots, 1, nx * ny), F32),
        ]
        return (
            faces
            + faces
            + [
                pltpu.VMEM((nx, ny + 16, nz), F32),
                pltpu.SemaphoreType.DMA((turns, 3, 2)),
                pltpu.SemaphoreType.DMA((turns, 3, 2)),
            ]
        )

    staged = [
        pltpu.VMEM(hshape, F32),
        pltpu.VMEM(hshape, F32),
        pltpu.VMEM(tshape, F32),
        pltpu.SemaphoreType.DMA((4,)),
    ] + [
        (pltpu.SMEM if number in in_smem else pltpu.VMEM)(array.shape, array.dtype)
        for number, array in enumerate(args)
    ] + [pltpu.SemaphoreType.DMA((len(args),))]
    patches = [pltpu.VMEM((peers, 1, cap), F32)] * 4
    signals = [pltpu.SemaphoreType.DMA((peers,))] * 4
    rows_h = hx // 4 * hy
    rows = tx // 4 * ty
    work = [
        pltpu.VMEM((2,) + hshape, F32),
        pltpu.VMEM((1,) + tshape, F32),
        pltpu.VMEM(tshape, F32),
        pltpu.VMEM(hshape, F32),
        pltpu.VMEM(hshape, F32),
        pltpu.VMEM(hshape, F32),
        pltpu.VMEM((6, tx, ty, tz), F32),
        pltpu.VMEM((tx // 4, ty, tz), F32),
        pltpu.VMEM((rows, tz), F32),
        pltpu.VMEM((peers, rows_h, cap), BF16),
        pltpu.VMEM((peers, 1, cap), jnp.int32),
        pltpu.VMEM((peers, rows, cap), BF16),
        pltpu.VMEM((peers, 1, cap), jnp.int32),
    ]
    shapes = tuple(jax.ShapeDtypeStruct(shape, F32) for shape in (hshape, hshape, tshape))
    results = pl.pallas_call(
        functools.partial(kernel, sizes),
        out_shape=shapes,
        in_specs=[hbm] * len(args),
        out_specs=(hbm, hbm, hbm),
        scratch_shapes=staged
        + grid_scratch(hshape, SWEEPS_H + 2, SWEEPS_H + 1)
        + grid_scratch(tshape, SWEEPS_T + 1, SWEEPS_T)
        + patches
        + signals
        + work,
        compiler_params=pltpu.CompilerParams(
            collective_id=0, has_side_effects=True, vmem_limit_bytes=64 * 1024 * 1024
        ),
    )(*args)
    return pl.pallas_call(
        write_out,
        out_shape=shapes,
        in_specs=[hbm, hbm, hbm],
        out_specs=(hbm, hbm, hbm),
        scratch_shapes=[pltpu.VMEM(array.shape, F32) for array in shapes]
        + [pltpu.SemaphoreType.DMA((2, 3))],
        compiler_params=pltpu.CompilerParams(vmem_limit_bytes=64 * 1024 * 1024),
    )(*results)


def solution(mesh):
    sizes = (mesh.shape["grp"], mesh.shape["gx"], mesh.shape["gy"])
    placed = (
        P(None, "gx", "gy", "grp"),
        P("gx", "gy", "grp"),
        P("gx", "gy", "grp"),
        P(),
        P("gx", "gy", "grp"),
        P("gx", "gy", "grp"),
        P("gx", "gy", "grp"),
        P(),
        P("grp", "gx", "gy", None, None),
        P("grp", "gx", "gy", None),
        P("grp", "gx", "gy", None, None),
        P("grp", "gx", "gy", None),
    )
    return jax.shard_map(
        functools.partial(per_device, sizes),
        mesh=mesh,
        in_specs=placed,
        out_specs=(P("gx", "gy", "grp"), P("gx", "gy", "grp"), P("gx", "gy", "grp")),
        check_vma=False,
    )
```

```python
import functools

import jax
import jax.numpy as jnp
from jax import lax
from jax.experimental import pallas as pl
from jax.experimental.pallas import tpu as pltpu
from jax.sharding import PartitionSpec as P

LABELS = 4
SWEEPS_H = 3
SWEEPS_T = 4

time_step = 0.1
intra_cond = 0.25
extra_cond = 0.5
penalty = 2.0
cheb_low = 0.1
cheb_high = 2.0

MESH = pl.DeviceIdType.MESH
F32 = jnp.float32
BF16 = jnp.bfloat16


def cheb_coeffs(sweeps):
    centre = 0.5 * (cheb_high + cheb_low)
    half_width = 0.5 * (cheb_high - cheb_low)
    scaled = centre / half_width
    coeffs = [(0.0, 1.0 / centre)]
    rho_old = 1.0 / scaled
    for number in range(1, sweeps):
        rho_new = 1.0 / (2.0 * scaled - rho_old)
        coeffs.append((rho_new * rho_old, 2.0 * rho_new / half_width))
        rho_old = rho_new
    return coeffs


def harmonic(a, b):
    return 2.0 * a * b / (a + b)


def two_terms(values):
    high = values.astype(BF16)
    return high, (values - high.astype(F32)).astype(BF16)


class Grid:
    def __init__(self, shape, stage, landing, sends, recvs, ypad, place, partial, ends, unroll):
        self.shape = shape
        self.stage = stage
        self.landing = landing
        self.sends = sends
        self.recvs = recvs
        self.ypad = ypad
        self.partial = partial
        self.ends = ends
        self.unroll = unroll
        self.place = place

    def clear_ends(self):
        self.clear_faces()
        for axis, (_, low, high) in enumerate(self.place):
            for side, (_, present) in enumerate((low, high)):
                if present is None:
                    continue

                @pl.when(jnp.logical_not(present))
                def _(axis=axis, side=side):
                    ref = self.landing[axis]
                    ref[side] = jnp.zeros(ref.shape[1:], F32)

    def pack(self, slot, field):
        nx, ny, nz = self.shape
        xs, ys, zs = self.stage
        xs[0, slot] = field[0]
        xs[1, slot] = field[nx - 1]
        ys[0, slot] = field[:, 0:1, :]
        ys[1, slot] = field[:, ny - 1 : ny, :]
        turned = jnp.transpose(field.reshape(nx * ny, nz))
        zs[0, slot] = turned[0:1, :]
        zs[1, slot] = turned[nz - 1 : nz, :]

    def copies(self, turn, first, count):
        for axis, (name, low, high) in enumerate(self.place):
            for side, there in enumerate((low, high)):
                back = (high, low)[side]
                yield (
                    pltpu.make_async_remote_copy(
                        src_ref=self.stage[axis].at[side, pl.ds(first, count)],
                        dst_ref=self.landing[axis].at[1 - side, pl.ds(first, count)],
                        send_sem=self.sends.at[turn, axis, side],
                        recv_sem=self.recvs.at[turn, axis, 1 - side],
                        device_id={name: there[0]},
                        device_id_type=MESH,
                    ),
                    there[1],
                    back[1],
                )

    def send(self, turn, first, count):
        for copy, out, _ in self.copies(turn, first, count):
            if out is None:
                copy.start()
            else:
                pl.when(out)(copy.start)

    def wait(self, turn, first, count):
        for copy, _, back in self.copies(turn, first, count):
            if back is None:
                copy.wait_recv()
            else:
                pl.when(back)(copy.wait_recv)

    def finish(self, turn, first, count):
        for copy, out, _ in self.copies(turn, first, count):
            if out is None:
                copy.wait_send()
            else:
                pl.when(out)(copy.wait_send)

    def planes(self, body):
        def one(at, carry):
            body(at)
            return carry

        lax.fori_loop(0, self.shape[0], one, 0, unroll=self.unroll)

    def get(self, at):
        return self.ypad[at + 1, 8 : 8 + self.shape[1], :]

    def put(self, at, plane):
        self.ypad[at + 1, 8 : 8 + self.shape[1], :] = plane

    def field(self):
        nx, ny, _ = self.shape
        return self.ypad[1 : nx + 1, 8 : 8 + ny, :]

    def inside(self, at):
        _, ny, nz = self.shape
        lanes = lax.broadcasted_iota(jnp.int32, (ny, nz), 1)
        plane = self.get(at)
        return [
            self.get(at - 1),
            self.get(at + 1),
            self.ypad[at + 1, 7 : 7 + ny, :],
            self.ypad[at + 1, 9 : 9 + ny, :],
            jnp.where(lanes == 0, 0.0, pltpu.roll(plane, 1, 1)),
            jnp.where(lanes == nz - 1, 0.0, pltpu.roll(plane, nz - 1, 1)),
        ]

    def begin(self, gains=None, which=0):
        def body(at):
            parts = self.inside(at)
            if gains is not None:
                parts = [gains[number, at] * part for number, part in enumerate(parts)]
            self.partial[which, at] = total_of(parts)

        self.planes(body)

    def turn_ends(self, slot):
        nx, ny, nz = self.shape
        rz = self.landing[2]
        depth = lax.broadcasted_iota(jnp.int32, (nz, nx * ny), 0)
        turned = jnp.where(depth == 0, rz[0, slot], jnp.where(depth == nz - 1, rz[1, slot], 0.0))
        self.ends[...] = jnp.transpose(turned).reshape(nx, ny, nz)

    def complete(self, slot, gains=None, which=0):
        nx, ny, nz = self.shape
        rx, ry, _ = self.landing
        self.turn_ends(slot)
        for side, at in ((0, 0), (1, nx - 1)):
            other = rx[side, slot]
            if gains is not None:
                other = gains[side, at] * other
            self.partial[which, at] = self.partial[which, at] + other
        for side, at in ((0, 0), (1, ny - 1)):
            other = ry[side, slot]
            if gains is not None:
                other = gains[2 + side, :, at : at + 1, :] * other
            self.partial[which, :, at : at + 1, :] = self.partial[which, :, at : at + 1, :] + other

    def pad_faces(self, slot):
        nx, ny, _ = self.shape
        rx, ry, _ = self.landing
        self.ypad[0, 8 : 8 + ny, :] = rx[0, slot]
        self.ypad[nx + 1, 8 : 8 + ny, :] = rx[1, slot]
        self.ypad[1 : nx + 1, 7:8, :] = ry[0, slot]
        self.ypad[1 : nx + 1, 8 + ny : 9 + ny, :] = ry[1, slot]

    def clear_faces(self):
        nx, ny, nz = self.shape
        self.ypad[0] = jnp.zeros((ny + 16, nz), F32)
        self.ypad[nx + 1] = jnp.zeros((ny + 16, nz), F32)
        self.ypad[1 : nx + 1, 7:8, :] = jnp.zeros((nx, 1, nz), F32)
        self.ypad[1 : nx + 1, 8 + ny : 9 + ny, :] = jnp.zeros((nx, 1, nz), F32)


def total_of(parts):
    return ((parts[0] + parts[1]) + (parts[2] + parts[3])) + (parts[4] + parts[5])


def turned_table(layer, rows, width):
    high, low = two_terms(jnp.transpose(layer.reshape(rows, width)))
    return jnp.concatenate([high, low], axis=1)


class Patch:
    def __init__(self, nodes, counts, row_hots, columns, rows, width):
        self.nodes = nodes
        self.counts = counts
        self.row_hots = row_hots
        self.columns = columns
        self.rows = rows
        self.width = width
        self.cap = nodes.shape[1]

    def prepare(self, peer):
        index = self.nodes[pl.ds(peer, 1), :]
        slot_ids = lax.broadcasted_iota(jnp.int32, (1, self.cap), 1)
        index = jnp.where(slot_ids < self.counts[peer], index, -1)
        row_ids = lax.broadcasted_iota(jnp.int32, (self.rows, self.cap), 0)
        row = lax.shift_right_arithmetic(index, self.width.bit_length() - 1)
        self.row_hots[peer] = jnp.where(row_ids == row, 1.0, 0.0).astype(BF16)
        self.columns[peer] = index & (self.width - 1)

    def column_mask(self, peer):
        col_ids = lax.broadcasted_iota(jnp.int32, (self.width, self.cap), 0)
        return col_ids == self.columns[peer]

    def pick(self, table, peer):
        row_hot = self.row_hots[peer]
        chosen = jnp.dot(
            table, jnp.concatenate([row_hot, row_hot], axis=0), preferred_element_type=F32
        )
        return jnp.sum(jnp.where(self.column_mask(peer), chosen, 0.0), axis=0, keepdims=True)

    def weigh(self, peer):
        ones = jnp.where(self.column_mask(peer), 1.0, 0.0).astype(BF16)
        return lax.dot_general(
            self.row_hots[peer], ones, (((1,), (1,)), ((), ())), preferred_element_type=F32
        )

    def place_at(self, values, peer):
        mask = self.column_mask(peer)
        high = values.astype(BF16).astype(F32)
        low = values - high
        spread = jnp.concatenate(
            [jnp.where(mask, high, 0.0).astype(BF16), jnp.where(mask, low, 0.0).astype(BF16)],
            axis=0,
        )
        return lax.dot_general(
            self.row_hots[peer], spread, (((1,), (1,)), ((), ())), preferred_element_type=F32
        )


def kernel(
    sizes,
    states_in,
    membrane_in,
    phi_heart_in,
    ion_params_in,
    torso_phi_in,
    tissue_scale_in,
    labels_in,
    cond_table_in,
    send_node_in,
    send_count_in,
    recv_voxel_in,
    recv_count_in,
    new_membrane_out,
    heart_phi_out,
    torso_out_out,
    new_membrane, heart_phi, torso_out, store_sem,
    states, membrane, phi_heart, ion_params, torso_phi, tissue_scale, labels, cond_table,
    send_node, send_count, recv_voxel, recv_count, load_sem,
    hsx, hsy, hsz, hrx, hry, hrz, hypad, hsend, hrecv,
    tsx, tsy, tsz, trx, try_, trz, typad, tsend, trecv,
    sent, arrived, returned, came,
    out_sem, in_sem, back_sem, home_sem,
    hpart, hends, update_h, tpart, tends, update_t, end_gain, conduct, phi_h, source_h,
    current_h, gains, right_t, weight_t,
    rows_node, cols_node, rows_voxel, cols_voxel,
):
    n_grp, n_gx, n_gy = sizes
    peers = n_gx * n_gy
    group = 2 if peers % 2 == 0 else 1
    g = lax.axis_index("grp")
    i = lax.axis_index("gx")
    j = lax.axis_index("gy")
    me = i * n_gy + j
    hshape = membrane.shape
    tshape = torso_phi.shape

    sources = (
        (membrane_in, membrane), (phi_heart_in, phi_heart), (tissue_scale_in, tissue_scale),
        (labels_in, labels), (cond_table_in, cond_table), (torso_phi_in, torso_phi),
        (ion_params_in, ion_params), (states_in, states), (send_node_in, send_node),
        (send_count_in, send_count), (recv_voxel_in, recv_voxel), (recv_count_in, recv_count),
    )
    layer_h = hshape[0] // 4
    surface = pl.ds(0, layer_h)
    deep = pl.ds(layer_h, hshape[0] - layer_h)
    stores = [
        pltpu.make_async_copy(new_membrane, new_membrane_out, store_sem.at[0]),
        pltpu.make_async_copy(torso_out, torso_out_out, store_sem.at[1]),
        pltpu.make_async_copy(heart_phi.at[deep], heart_phi_out.at[deep], store_sem.at[2]),
        pltpu.make_async_copy(heart_phi.at[surface], heart_phi_out.at[surface], store_sem.at[3]),
    ]
    loads = [
        pltpu.make_async_copy(there, here, load_sem.at[number])
        for number, (there, here) in enumerate(sources)
    ]
    for load in loads:
        load.start()

    place = (
        ("gx", (lax.rem(i + n_gx - 1, n_gx), None), (lax.rem(i + 1, n_gx), None)),
        ("gy", (jnp.maximum(j - 1, 0), j > 0), (jnp.minimum(j + 1, n_gy - 1), j < n_gy - 1)),
        ("grp", (jnp.maximum(g - 1, 0), g > 0), (jnp.minimum(g + 1, n_grp - 1), g < n_grp - 1)),
    )
    heart = Grid(hshape, (hsx, hsy, hsz), (hrx, hry, hrz), hsend, hrecv, hypad, place, hpart, hends, 4)
    torso = Grid(tshape, (tsx, tsy, tsz), (trx, try_, trz), tsend, trecv, typad, place, tpart, tends, 2)
    heart.clear_ends()
    torso.clear_ends()

    def peer_at(step):
        other = lax.rem(me + step, peers)
        return other, {"gx": other // n_gy, "gy": lax.rem(other, n_gy)}

    barrier = pltpu.get_barrier_semaphore()

    def greet(step, carry):
        pl.semaphore_signal(barrier, inc=1, device_id=peer_at(step)[1], device_id_type=MESH)
        return carry

    lax.fori_loop(1, peers, greet, 0, unroll=peers <= 8)
    _, low_z, high_z = place[2]
    for there, present in (low_z, high_z):

        @pl.when(present)
        def _(there=there):
            pl.semaphore_signal(barrier, inc=1, device_id={"grp": there}, device_id_type=MESH)

    loads[0].wait()
    heart.pack(0, membrane[...])
    loads[1].wait()
    heart.pack(1, phi_heart[...])
    pl.semaphore_wait(
        barrier, peers - 1 + (g > 0).astype(jnp.int32) + (g < n_grp - 1).astype(jnp.int32)
    )
    heart.send(0, 0, 2)

    for load in loads[2:6]:
        load.wait()

    def conductivity(at):
        names = labels[at]
        table = jnp.where(names == 0, cond_table[0], 0.0)
        for number in range(1, LABELS):
            table = jnp.where(names == number, cond_table[number], table)
        conduct[at] = tissue_scale[at] * table

    torso.planes(conductivity)
    torso.pack(0, conduct[...])
    torso.pack(1, torso_phi[...])
    torso.send(0, 0, 2)

    def ionic(first, last):
        line = jnp.zeros((1, hshape[2]), F32)
        half_slopes = [0.5 / (line + ion_params[1, state]) for state in range(first, last)]
        decays = [jnp.exp(line - time_step * ion_params[2, state]) for state in range(first, last)]

        def body(at):
            voltage = membrane[at]
            current = jnp.zeros(hshape[1:], F32) if first == 0 else current_h[at]
            for state in range(first, last):
                half_slope, decay = half_slopes[state - first], decays[state - first]
                steady = 0.5 + 0.5 * jnp.tanh((voltage - ion_params[0, state]) * half_slope)
                gate = steady + (states[state, at].astype(F32) - steady) * decay
                current = current + ion_params[3, state] * gate * (voltage - ion_params[4, state])
            current_h[at] = current

        heart.planes(body)

    def fill(grid, ref):
        grid.planes(lambda at: grid.put(at, ref[at]))

    fill(heart, membrane)
    heart.begin(which=0)
    fill(heart, phi_heart)
    heart.begin(which=1)

    ny = lax.broadcasted_iota(jnp.int32, hshape[1:], 0) + j * hshape[1]
    nz = lax.broadcasted_iota(jnp.int32, hshape[1:], 1) + g * hshape[2]
    diag = (
        6.0
        - jnp.where(ny == 0, 1.0, 0.0)
        - jnp.where(ny == hshape[1] * n_gy - 1, 1.0, 0.0)
        - jnp.where(nz == 0, 1.0, 0.0)
        - jnp.where(nz == hshape[2] * n_grp - 1, 1.0, 0.0)
    )
    inverse = 1.0 / diag

    rows_h = layer_h * hshape[1]
    layer = tshape[0] // 4
    rows = layer * tshape[1]
    width = tshape[2]
    nodes = Patch(send_node, send_count, rows_node, cols_node, rows_h, hshape[2])
    voxels = Patch(recv_voxel, recv_count, rows_voxel, cols_voxel, rows, width)

    def over_peers(body, start):
        def one_group(number, carry):
            for offset in range(group):
                carry = body(number * group + offset, carry)
            return carry

        return lax.fori_loop(0, peers // group, one_group, start)

    def indices():
        for load in loads[8:]:
            load.wait()

        def prepare(peer, carry):
            nodes.prepare(peer)
            voxels.prepare(peer)
            return carry + voxels.weigh(peer)

        weight = penalty * over_peers(prepare, jnp.zeros((rows, width), F32))
        weight_t[0:layer] = weight.reshape(layer, tshape[1], width)
        weight_t[layer:] = jnp.zeros((tshape[0] - layer,) + tshape[1:], F32)

    def conductances():
        fill(torso, conduct)
        torso.wait(0, 0, 2)
        torso.pad_faces(0)
        torso.turn_ends(0)
        lanes = lax.broadcasted_iota(jnp.int32, tshape[1:], 1)

        def body(at):
            plane = conduct[at]
            ends = torso.ends[at]
            parts = torso.inside(at)
            parts[4] = parts[4] + jnp.where(lanes == 0, ends, 0.0)
            parts[5] = parts[5] + jnp.where(lanes == width - 1, ends, 0.0)
            faces = [harmonic(plane, part) for part in parts]
            scale = 1.0 / (total_of(faces) + weight_t[at])
            for number in range(6):
                gains[number, at] = faces[number] * scale
            end_gain[at] = jnp.where(
                lanes == 0, faces[4] * scale, jnp.where(lanes == width - 1, faces[5] * scale, 0.0)
            )
            right_t[at] = penalty * scale

        torso.planes(body)
        torso.clear_faces()

    indices()
    heart.wait(0, 0, 2)
    heart.complete(0, which=0)

    def laplacian(at):
        source_h[at] = diag * membrane[at] - (heart.partial[0, at] + heart.ends[at])

    heart.planes(laplacian)
    from_lap = (-intra_cond / (intra_cond + extra_cond)) * inverse
    for number, (carry_coef, resid_coef) in enumerate(cheb_coeffs(SWEEPS_H)):
        if number > 0:
            heart.wait(number, number + 1, 1)
        heart.complete(number + 1, which=1)

        def sweep(at, number=number, carry_coef=carry_coef, resid_coef=resid_coef):
            iterate = heart.get(at)
            around = heart.partial[1, at] + heart.ends[at]
            residue = source_h[at] * from_lap - iterate + around * inverse
            update = resid_coef * residue
            if number > 0:
                update = carry_coef * update_h[at] + update
            update_h[at] = update
            iterate = iterate + update
            heart.put(at, iterate)
            if number == SWEEPS_H - 1:
                phi_h[at] = iterate

        heart.planes(sweep)
        if number < SWEEPS_H - 1:
            heart.pack(number + 2, heart.field())
            heart.send(number + 1, number + 2, 1)
            heart.begin(which=1)
        if number == 0:
            conductances()
        if number == 1:
            fill(torso, torso_phi)
            torso.begin(gains)
            torso.complete(1, gains)

    def patch(other, source, target, sends, recvs, mine):
        return pltpu.make_async_remote_copy(
            src_ref=source.at[other],
            dst_ref=target.at[mine],
            send_sem=sends.at[other],
            recv_sem=recvs.at[mine],
            device_id={"gx": other // n_gy, "gy": lax.rem(other, n_gy)},
            device_id_type=MESH,
        )

    to_torso = (sent, arrived, out_sem, in_sem)
    to_heart = (returned, came, back_sem, home_sem)

    def post(buffers, fill):
        source, target = buffers[:2]

        def one_group(number, carry):
            picked = [fill(number * group + offset) for offset in range(group)]
            for offset in range(group):
                source[number * group + offset] = picked[offset]
            return carry

        lax.fori_loop(0, peers // group, one_group, 0)

        def start(step, carry):
            patch(peer_at(step)[0], *buffers, me).start()
            return carry

        lax.fori_loop(1, peers, start, 0, unroll=peers <= 8)
        target[me] = source[me]

    def receive(buffers):
        def land(step, carry):
            other = peer_at(step)[0]
            patch(other, *buffers, other).wait_recv()
            return carry

        lax.fori_loop(1, peers, land, 0, unroll=peers <= 8)

    table_h = turned_table(phi_h[0:layer_h], rows_h, hshape[2])
    post(to_torso, lambda peer: nodes.pick(table_h, peer))
    heart.pack(SWEEPS_H + 1, phi_h[...])
    heart.send(SWEEPS_H, SWEEPS_H + 1, 1)

    heart.begin(which=1)
    half = states.shape[0] // 2
    loads[6].wait()
    loads[7].wait()
    ionic(0, half)
    receive(to_torso)
    summed = over_peers(
        lambda peer, carry: carry + voxels.place_at(arrived[peer], peer),
        jnp.zeros((rows, 2 * width), F32),
    )
    summed = summed[:, :width] + summed[:, width:]
    right_t[0:layer] = summed.reshape(layer, tshape[1], width) * right_t[0:layer]
    right_t[layer:] = jnp.zeros((tshape[0] - layer,) + tshape[1:], F32)

    for number, (carry_coef, resid_coef) in enumerate(cheb_coeffs(SWEEPS_T)):
        if number > 0:
            torso.pack(number + 1, torso.field())
            torso.send(number, number + 1, 1)
            torso.begin(gains)
        if number == 1:
            ionic(half, states.shape[0])
        if number == 2:
            heart.wait(SWEEPS_H, SWEEPS_H + 1, 1)
            heart.complete(SWEEPS_H + 1, which=1)

            def depolarise(at):
                lap_phi = diag * phi_h[at] - (heart.partial[1, at] + heart.ends[at])
                new_membrane[at] = membrane[at] + time_step * (
                    -intra_cond * (source_h[at] + lap_phi) - current_h[at]
                )

            heart.planes(depolarise)
            stores[0].start()
        if number == SWEEPS_T - 1:
            heart_phi[layer_h:] = phi_h[layer_h:]
            stores[2].start()
        if number > 0:
            torso.wait(number, number + 1, 1)
            torso.complete(number + 1, gains)

        def sweep_t(at, number=number, carry_coef=carry_coef, resid_coef=resid_coef):
            iterate = torso.get(at)
            around = torso.partial[0, at] + end_gain[at] * torso.ends[at]
            update = resid_coef * (right_t[at] + (around - iterate))
            if number > 0:
                update = carry_coef * update_t[at] + update
            update_t[at] = update
            iterate = iterate + update
            torso.put(at, iterate)
            if number == SWEEPS_T - 1:
                torso_out[at] = iterate

        torso.planes(sweep_t)
    table_t = turned_table(torso_out[0:layer], rows, width)
    post(
        to_heart, lambda peer: penalty * (arrived[peer] - voxels.pick(table_t, peer))
    )
    stores[1].start()

    heart.finish(0, 0, 2)
    torso.finish(0, 0, 2)
    for number in range(1, SWEEPS_H + 1):
        heart.finish(number, number + 1, 1)
    for number in range(1, SWEEPS_T):
        torso.finish(number, number + 1, 1)

    receive(to_heart)
    flux = over_peers(
        lambda peer, carry: carry + nodes.place_at(came[peer], peer),
        jnp.zeros((rows_h, 2 * hshape[2]), F32),
    )
    flux = (flux[:, : hshape[2]] + flux[:, hshape[2] :]).reshape(layer_h, hshape[1], hshape[2])
    heart_phi[0:layer_h] = phi_h[0:layer_h] - flux * (
        inverse * (1.0 / (intra_cond + extra_cond))
    )
    stores[3].start()

    def settle(step, carry):
        other = peer_at(step)[0]
        patch(other, *to_torso, other).wait_send()
        patch(other, *to_heart, other).wait_send()
        return carry

    lax.fori_loop(1, peers, settle, 0, unroll=peers <= 8)
    for store in stores:
        store.wait()


def write_out(*refs):
    sources, targets, held, (sems,) = refs[:3], refs[3:6], refs[6:9], refs[9:]
    ins = [
        pltpu.make_async_copy(there, here, sems.at[0, number])
        for number, (there, here) in enumerate(zip(sources, held))
    ]
    outs = [
        pltpu.make_async_copy(here, there, sems.at[1, number])
        for number, (here, there) in enumerate(zip(held, targets))
    ]
    for copy in ins:
        copy.start()
    for copy, after in zip(ins, outs):
        copy.wait()
        after.start()
    for copy in outs:
        copy.wait()


def per_device(sizes, *args):
    peers, cap = args[8].shape[-2:]
    args = list(args)
    for number in (8, 10):
        args[number] = args[number].reshape(peers, cap)
    for number in (9, 11):
        args[number] = args[number].reshape(peers)
    hshape = args[1].shape
    tshape = args[4].shape
    hx, hy, hz = hshape
    tx, ty, tz = tshape
    hbm = pl.BlockSpec(memory_space=pltpu.HBM)
    in_smem = (3, 7, 9, 11)

    def grid_scratch(shape, slots, turns):
        nx, ny, nz = shape
        faces = [
            pltpu.VMEM((2, slots, ny, nz), F32),
            pltpu.VMEM((2, slots, nx, 1, nz), F32),
            pltpu.VMEM((2, slots, 1, nx * ny), F32),
        ]
        return (
            faces
            + faces
            + [
                pltpu.VMEM((nx + 2, ny + 16, nz), F32),
                pltpu.SemaphoreType.DMA((turns, 3, 2)),
                pltpu.SemaphoreType.DMA((turns, 3, 2)),
            ]
        )

    staged = [
        pltpu.VMEM(hshape, F32),
        pltpu.VMEM(hshape, F32),
        pltpu.VMEM(tshape, F32),
        pltpu.SemaphoreType.DMA((4,)),
    ] + [
        (pltpu.SMEM if number in in_smem else pltpu.VMEM)(array.shape, array.dtype)
        for number, array in enumerate(args)
    ] + [pltpu.SemaphoreType.DMA((len(args),))]
    patches = [pltpu.VMEM((peers, 1, cap), F32)] * 4
    signals = [pltpu.SemaphoreType.DMA((peers,))] * 4
    rows_h = hx // 4 * hy
    rows = tx // 4 * ty
    work = [
        pltpu.VMEM((2,) + hshape, F32),
        pltpu.VMEM(hshape, F32),
        pltpu.VMEM(hshape, F32),
        pltpu.VMEM((1,) + tshape, F32),
        pltpu.VMEM(tshape, F32),
        pltpu.VMEM(tshape, F32),
        pltpu.VMEM(tshape, F32),
        pltpu.VMEM(tshape, F32),
        pltpu.VMEM(hshape, F32),
        pltpu.VMEM(hshape, F32),
        pltpu.VMEM(hshape, F32),
        pltpu.VMEM((6, tx, ty, tz), F32),
        pltpu.VMEM(tshape, F32),
        pltpu.VMEM(tshape, F32),
        pltpu.VMEM((peers, rows_h, cap), BF16),
        pltpu.VMEM((peers, 1, cap), jnp.int32),
        pltpu.VMEM((peers, rows, cap), BF16),
        pltpu.VMEM((peers, 1, cap), jnp.int32),
    ]
    shapes = tuple(jax.ShapeDtypeStruct(shape, F32) for shape in (hshape, hshape, tshape))
    results = pl.pallas_call(
        functools.partial(kernel, sizes),
        out_shape=shapes,
        in_specs=[hbm] * len(args),
        out_specs=(hbm, hbm, hbm),
        scratch_shapes=staged
        + grid_scratch(hshape, SWEEPS_H + 2, SWEEPS_H + 1)
        + grid_scratch(tshape, SWEEPS_T + 1, SWEEPS_T)
        + patches
        + signals
        + work,
        compiler_params=pltpu.CompilerParams(
            collective_id=0, has_side_effects=True, vmem_limit_bytes=64 * 1024 * 1024
        ),
    )(*args)
    return pl.pallas_call(
        write_out,
        out_shape=shapes,
        in_specs=[hbm, hbm, hbm],
        out_specs=(hbm, hbm, hbm),
        scratch_shapes=[pltpu.VMEM(array.shape, F32) for array in shapes]
        + [pltpu.SemaphoreType.DMA((2, 3))],
        compiler_params=pltpu.CompilerParams(vmem_limit_bytes=64 * 1024 * 1024),
    )(*results)


def solution(mesh):
    sizes = (mesh.shape["grp"], mesh.shape["gx"], mesh.shape["gy"])
    placed = (
        P(None, "gx", "gy", "grp"),
        P("gx", "gy", "grp"),
        P("gx", "gy", "grp"),
        P(),
        P("gx", "gy", "grp"),
        P("gx", "gy", "grp"),
        P("gx", "gy", "grp"),
        P(),
        P("grp", "gx", "gy", None, None),
        P("grp", "gx", "gy", None),
        P("grp", "gx", "gy", None, None),
        P("grp", "gx", "gy", None),
    )
    return jax.shard_map(
        functools.partial(per_device, sizes),
        mesh=mesh,
        in_specs=placed,
        out_specs=(P("gx", "gy", "grp"), P("gx", "gy", "grp"), P("gx", "gy", "grp")),
        check_vma=False,
    )
```

```python
import functools

import jax
import jax.numpy as jnp
from jax import lax
from jax.experimental import pallas as pl
from jax.experimental.pallas import tpu as pltpu
from jax.sharding import PartitionSpec as P

LABELS = 4
SWEEPS_H = 3
SWEEPS_T = 4

time_step = 0.1
intra_cond = 0.25
extra_cond = 0.5
penalty = 2.0
cheb_low = 0.1
cheb_high = 2.0

MESH = pl.DeviceIdType.MESH
F32 = jnp.float32
BF16 = jnp.bfloat16


def cheb_coeffs(sweeps):
    centre = 0.5 * (cheb_high + cheb_low)
    half_width = 0.5 * (cheb_high - cheb_low)
    scaled = centre / half_width
    coeffs = [(0.0, 1.0 / centre)]
    rho_old = 1.0 / scaled
    for number in range(1, sweeps):
        rho_new = 1.0 / (2.0 * scaled - rho_old)
        coeffs.append((rho_new * rho_old, 2.0 * rho_new / half_width))
        rho_old = rho_new
    return coeffs


def harmonic(a, b):
    return 2.0 * a * b / (a + b)


def two_terms(values):
    high = values.astype(BF16)
    return high, (values - high.astype(F32)).astype(BF16)


class Grid:
    def __init__(self, shape, stage, landing, sends, recvs, ypad, place, partial):
        self.shape = shape
        self.stage = stage
        self.landing = landing
        self.sends = sends
        self.recvs = recvs
        self.ypad = ypad
        self.partial = partial
        self.place = place

    def clear_ends(self):
        nx, ny, nz = self.shape
        self.ypad[:, 7:8, :] = jnp.zeros((nx, 1, nz), F32)
        self.ypad[:, 8 + ny : 9 + ny, :] = jnp.zeros((nx, 1, nz), F32)
        for axis, (_, low, high) in enumerate(self.place):
            for side, (_, present) in enumerate((low, high)):
                if present is None:
                    continue

                @pl.when(jnp.logical_not(present))
                def _(axis=axis, side=side):
                    ref = self.landing[axis]
                    ref[side] = jnp.zeros(ref.shape[1:], F32)

    def pack(self, slot, field):
        nx, ny, nz = self.shape
        xs, ys, zs = self.stage
        xs[0, slot] = field[0]
        xs[1, slot] = field[nx - 1]
        ys[0, slot] = field[:, 0:1, :]
        ys[1, slot] = field[:, ny - 1 : ny, :]
        turned = jnp.transpose(field.reshape(nx * ny, nz))
        zs[0, slot] = turned[0:1, :]
        zs[1, slot] = turned[nz - 1 : nz, :]

    def copies(self, turn, first, count):
        for axis, (name, low, high) in enumerate(self.place):
            for side, there in enumerate((low, high)):
                back = (high, low)[side]
                yield (
                    pltpu.make_async_remote_copy(
                        src_ref=self.stage[axis].at[side, pl.ds(first, count)],
                        dst_ref=self.landing[axis].at[1 - side, pl.ds(first, count)],
                        send_sem=self.sends.at[turn, axis, side],
                        recv_sem=self.recvs.at[turn, axis, 1 - side],
                        device_id={name: there[0]},
                        device_id_type=MESH,
                    ),
                    there[1],
                    back[1],
                )

    def send(self, turn, first, count):
        for copy, out, _ in self.copies(turn, first, count):
            if out is None:
                copy.start()
            else:
                pl.when(out)(copy.start)

    def wait(self, turn, first, count):
        for copy, _, back in self.copies(turn, first, count):
            if back is None:
                copy.wait_recv()
            else:
                pl.when(back)(copy.wait_recv)

    def finish(self, turn, first, count):
        for copy, out, _ in self.copies(turn, first, count):
            if out is None:
                copy.wait_send()
            else:
                pl.when(out)(copy.wait_send)

    def inside(self, field):
        nx, ny, nz = self.shape
        none = jnp.zeros((1, ny, nz), F32)
        below_x = jnp.concatenate([none, field[:-1]], axis=0)
        above_x = jnp.concatenate([field[1:], none], axis=0)
        self.ypad[:, 8 : 8 + ny, :] = field
        below_y = self.ypad[:, 7 : 7 + ny, :]
        above_y = self.ypad[:, 9 : 9 + ny, :]
        flat = field.reshape(nx * ny, nz)
        lanes = lax.broadcasted_iota(jnp.int32, (nx * ny, nz), 1)
        below_z = jnp.where(lanes == 0, 0.0, pltpu.roll(flat, 1, 1)).reshape(nx, ny, nz)
        above_z = jnp.where(lanes == nz - 1, 0.0, pltpu.roll(flat, nz - 1, 1)).reshape(nx, ny, nz)
        return below_x, above_x, below_y, above_y, below_z, above_z

    def begin(self, field, gains=None, which=0):
        parts = self.inside(field)
        if gains is not None:
            parts = [gains[number] * part for number, part in enumerate(parts)]
        self.partial[which] = total_of(parts)

    def ends(self, slot):
        nx, ny, nz = self.shape
        rz = self.landing[2]
        depth = lax.broadcasted_iota(jnp.int32, (nz, nx * ny), 0)
        turned = jnp.where(depth == 0, rz[0, slot], jnp.where(depth == nz - 1, rz[1, slot], 0.0))
        return jnp.transpose(turned).reshape(nx, ny, nz)

    def complete(self, slot, gains=None, end_gain=None, which=0):
        nx, ny, nz = self.shape
        rx, ry, _ = self.landing
        ends = self.ends(slot)
        for side, at in ((0, 0), (1, nx - 1)):
            other = rx[side, slot]
            if gains is not None:
                other = gains[side, at] * other
            self.partial[which, at] = self.partial[which, at] + other
        for side, at in ((0, 0), (1, ny - 1)):
            other = ry[side, slot]
            if gains is not None:
                other = gains[2 + side, :, at : at + 1, :] * other
            self.partial[which, :, at : at + 1, :] = self.partial[which, :, at : at + 1, :] + other
        if end_gain is not None:
            ends = end_gain[...] * ends
        return self.partial[which] + ends

    def around(self, slot, field):
        nx, ny, nz = self.shape
        rx, ry, _ = self.landing
        below_x, above_x, below_y, above_y, below_z, above_z = self.inside(field)
        below_x = jnp.concatenate([rx[0, slot][None], below_x[1:]], axis=0)
        above_x = jnp.concatenate([above_x[:-1], rx[1, slot][None]], axis=0)
        rows = lax.broadcasted_iota(jnp.int32, (nx, ny, nz), 1)
        below_y = jnp.where(rows == 0, ry[0, slot], below_y)
        above_y = jnp.where(rows == ny - 1, ry[1, slot], above_y)
        lanes = lax.broadcasted_iota(jnp.int32, (nx, ny, nz), 2)
        ends = self.ends(slot)
        below_z = jnp.where(lanes == 0, ends, below_z)
        above_z = jnp.where(lanes == nz - 1, ends, above_z)
        return below_x, above_x, below_y, above_y, below_z, above_z


def total_of(parts):
    return ((parts[0] + parts[1]) + (parts[2] + parts[3])) + (parts[4] + parts[5])


def turned_table(layer, rows, width):
    high, low = two_terms(jnp.transpose(layer.reshape(rows, width)))
    return jnp.concatenate([high, low], axis=1)


class Patch:
    def __init__(self, nodes, counts, row_hots, columns, rows, width):
        self.nodes = nodes
        self.counts = counts
        self.row_hots = row_hots
        self.columns = columns
        self.rows = rows
        self.width = width
        self.cap = nodes.shape[1]

    def prepare(self, peer):
        index = self.nodes[pl.ds(peer, 1), :]
        slot_ids = lax.broadcasted_iota(jnp.int32, (1, self.cap), 1)
        index = jnp.where(slot_ids < self.counts[peer], index, -1)
        row_ids = lax.broadcasted_iota(jnp.int32, (self.rows, self.cap), 0)
        row = lax.shift_right_arithmetic(index, self.width.bit_length() - 1)
        self.row_hots[peer] = jnp.where(row_ids == row, 1.0, 0.0).astype(BF16)
        self.columns[peer] = index & (self.width - 1)

    def column_mask(self, peer):
        col_ids = lax.broadcasted_iota(jnp.int32, (self.width, self.cap), 0)
        return col_ids == self.columns[peer]

    def pick(self, table, peer):
        row_hot = self.row_hots[peer]
        chosen = jnp.dot(
            table, jnp.concatenate([row_hot, row_hot], axis=0), preferred_element_type=F32
        )
        return jnp.sum(jnp.where(self.column_mask(peer), chosen, 0.0), axis=0, keepdims=True)

    def weigh(self, peer):
        ones = jnp.where(self.column_mask(peer), 1.0, 0.0).astype(BF16)
        return lax.dot_general(
            self.row_hots[peer], ones, (((1,), (1,)), ((), ())), preferred_element_type=F32
        )

    def place_at(self, values, peer):
        mask = self.column_mask(peer)
        high = values.astype(BF16).astype(F32)
        low = values - high
        spread = jnp.concatenate(
            [jnp.where(mask, high, 0.0).astype(BF16), jnp.where(mask, low, 0.0).astype(BF16)],
            axis=0,
        )
        return lax.dot_general(
            self.row_hots[peer], spread, (((1,), (1,)), ((), ())), preferred_element_type=F32
        )


def kernel(
    sizes,
    states_in,
    membrane_in,
    phi_heart_in,
    ion_params_in,
    torso_phi_in,
    tissue_scale_in,
    labels_in,
    cond_table_in,
    send_node_in,
    send_count_in,
    recv_voxel_in,
    recv_count_in,
    new_membrane_out,
    heart_phi_out,
    torso_out_out,
    new_membrane, heart_phi, torso_out, store_sem,
    states, membrane, phi_heart, ion_params, torso_phi, tissue_scale, labels, cond_table,
    send_node, send_count, recv_voxel, recv_count, load_sem,
    hsx, hsy, hsz, hrx, hry, hrz, hypad, hsend, hrecv,
    tsx, tsy, tsz, trx, try_, trz, typad, tsend, trecv,
    sent, arrived, returned, came,
    out_sem, in_sem, back_sem, home_sem,
    hpart, tpart, end_gain, phi_h, source_h, current_h, gains, right_t, weight_t,
    rows_node, cols_node, rows_voxel, cols_voxel,
):
    n_grp, n_gx, n_gy = sizes
    peers = n_gx * n_gy
    group = 8 if peers % 8 == 0 else 1
    g = lax.axis_index("grp")
    i = lax.axis_index("gx")
    j = lax.axis_index("gy")
    me = i * n_gy + j
    hshape = membrane.shape
    tshape = torso_phi.shape

    sources = (
        (membrane_in, membrane), (phi_heart_in, phi_heart), (tissue_scale_in, tissue_scale),
        (labels_in, labels), (cond_table_in, cond_table), (torso_phi_in, torso_phi),
        (ion_params_in, ion_params), (states_in, states), (send_node_in, send_node),
        (send_count_in, send_count), (recv_voxel_in, recv_voxel), (recv_count_in, recv_count),
    )
    layer_h = hshape[0] // 4
    surface = pl.ds(0, layer_h)
    deep = pl.ds(layer_h, hshape[0] - layer_h)
    stores = [
        pltpu.make_async_copy(new_membrane, new_membrane_out, store_sem.at[0]),
        pltpu.make_async_copy(torso_out, torso_out_out, store_sem.at[1]),
        pltpu.make_async_copy(heart_phi.at[deep], heart_phi_out.at[deep], store_sem.at[2]),
        pltpu.make_async_copy(heart_phi.at[surface], heart_phi_out.at[surface], store_sem.at[3]),
    ]
    loads = [
        pltpu.make_async_copy(there, here, load_sem.at[number])
        for number, (there, here) in enumerate(sources)
    ]
    for load in loads:
        load.start()

    place = (
        ("gx", (lax.rem(i + n_gx - 1, n_gx), None), (lax.rem(i + 1, n_gx), None)),
        ("gy", (jnp.maximum(j - 1, 0), j > 0), (jnp.minimum(j + 1, n_gy - 1), j < n_gy - 1)),
        ("grp", (jnp.maximum(g - 1, 0), g > 0), (jnp.minimum(g + 1, n_grp - 1), g < n_grp - 1)),
    )
    heart = Grid(hshape, (hsx, hsy, hsz), (hrx, hry, hrz), hsend, hrecv, hypad, place, hpart)
    torso = Grid(tshape, (tsx, tsy, tsz), (trx, try_, trz), tsend, trecv, typad, place, tpart)
    heart.clear_ends()
    torso.clear_ends()

    def peer_at(step):
        other = lax.rem(me + step, peers)
        return other, {"gx": other // n_gy, "gy": lax.rem(other, n_gy)}

    barrier = pltpu.get_barrier_semaphore()

    def greet(step, carry):
        pl.semaphore_signal(barrier, inc=1, device_id=peer_at(step)[1], device_id_type=MESH)
        return carry

    lax.fori_loop(1, peers, greet, 0, unroll=peers <= 8)
    _, low_z, high_z = place[2]
    for there, present in (low_z, high_z):

        @pl.when(present)
        def _(there=there):
            pl.semaphore_signal(barrier, inc=1, device_id={"grp": there}, device_id_type=MESH)

    loads[0].wait()
    voltage = membrane[...]
    heart.pack(0, voltage)
    loads[1].wait()
    heart.pack(1, phi_heart[...])
    pl.semaphore_wait(
        barrier, peers - 1 + (g > 0).astype(jnp.int32) + (g < n_grp - 1).astype(jnp.int32)
    )
    heart.send(0, 0, 2)

    for load in loads[2:6]:
        load.wait()
    names = labels[...]
    table = jnp.where(names == 0, cond_table[0], 0.0)
    for number in range(1, LABELS):
        table = jnp.where(names == number, cond_table[number], table)
    conduct = tissue_scale[...] * table
    torso.pack(0, conduct)
    torso.pack(1, torso_phi[...])
    torso.send(0, 0, 2)

    def ionic(first, last):
        voltage = membrane[...]
        current = jnp.zeros(hshape, F32) if first == 0 else current_h[...]
        for state in range(first, last):
            line = jnp.zeros((1, 1, hshape[2]), F32)
            half_slope = 0.5 / (line + ion_params[1, state])
            decay = jnp.exp(line - time_step * ion_params[2, state])
            steady = 0.5 + 0.5 * jnp.tanh((voltage - ion_params[0, state]) * half_slope)
            gate = steady + (states[state].astype(F32) - steady) * decay
            current = current + ion_params[3, state] * gate * (voltage - ion_params[4, state])
        current_h[...] = current

    heart.begin(voltage, which=0)
    heart.begin(phi_heart[...], which=1)

    ny = lax.broadcasted_iota(jnp.int32, hshape, 1) + j * hshape[1]
    nz = lax.broadcasted_iota(jnp.int32, hshape, 2) + g * hshape[2]
    diag = (
        6.0
        - jnp.where(ny == 0, 1.0, 0.0)
        - jnp.where(ny == hshape[1] * n_gy - 1, 1.0, 0.0)
        - jnp.where(nz == 0, 1.0, 0.0)
        - jnp.where(nz == hshape[2] * n_grp - 1, 1.0, 0.0)
    )
    inverse = 1.0 / diag

    rows_h = layer_h * hshape[1]
    layer = tshape[0] // 4
    rows = layer * tshape[1]
    width = tshape[2]
    nodes = Patch(send_node, send_count, rows_node, cols_node, rows_h, hshape[2])
    voxels = Patch(recv_voxel, recv_count, rows_voxel, cols_voxel, rows, width)

    def over_peers(body, start):
        def one_group(number, carry):
            for offset in range(group):
                carry = body(number * group + offset, carry)
            return carry

        if peers == group:
            return one_group(0, start)
        return lax.fori_loop(0, peers // group, one_group, start)

    def indices():
        for load in loads[8:]:
            load.wait()

        def prepare(peer, carry):
            nodes.prepare(peer)
            voxels.prepare(peer)
            return carry + voxels.weigh(peer)

        weight_t[...] = penalty * over_peers(prepare, jnp.zeros((rows, width), F32))

    def conductances():
        torso.wait(0, 0, 2)
        faces = [harmonic(conduct, other) for other in torso.around(0, conduct)]
        weight = weight_t[...].reshape(layer, tshape[1], width)
        total = total_of(faces)
        total = jnp.concatenate([total[:layer] + weight, total[layer:]], axis=0)
        scale = 1.0 / total
        for number in range(6):
            gains[number] = faces[number] * scale
        lanes = lax.broadcasted_iota(jnp.int32, tshape, 2)
        end_gain[...] = jnp.where(
            lanes == 0, faces[4] * scale, jnp.where(lanes == width - 1, faces[5] * scale, 0.0)
        )
        right_t[...] = penalty * scale[:layer]

    heart.wait(0, 0, 2)
    lap_mem = diag * voltage - heart.complete(0, which=0)
    source_h[...] = lap_mem
    base = (-intra_cond / (intra_cond + extra_cond)) * lap_mem * inverse
    iterate = phi_heart[...]
    update = None
    for number, (carry_coef, resid_coef) in enumerate(cheb_coeffs(SWEEPS_H)):
        if number > 0:
            heart.wait(number, number + 1, 1)
        around = heart.complete(number + 1, which=1)
        residue = base - iterate + around * inverse
        update = resid_coef * residue if update is None else carry_coef * update + resid_coef * residue
        iterate = iterate + update
        if number < SWEEPS_H - 1:
            heart.pack(number + 2, iterate)
            heart.send(number + 1, number + 2, 1)
            heart.begin(iterate, which=1)
        if number == 0:
            indices()
        if number == 1:
            conductances()
    phi_new = iterate
    phi_h[...] = phi_new

    def patch(other, source, target, sends, recvs, mine):
        return pltpu.make_async_remote_copy(
            src_ref=source.at[other],
            dst_ref=target.at[mine],
            send_sem=sends.at[other],
            recv_sem=recvs.at[mine],
            device_id={"gx": other // n_gy, "gy": lax.rem(other, n_gy)},
            device_id_type=MESH,
        )

    to_torso = (sent, arrived, out_sem, in_sem)
    to_heart = (returned, came, back_sem, home_sem)

    def post(buffers, fill):
        source, target = buffers[:2]

        def one_group(number, carry):
            picked = [fill(number * group + offset) for offset in range(group)]
            for offset in range(group):
                source[number * group + offset] = picked[offset]
            return carry

        if peers == group:
            one_group(0, 0)
        else:
            lax.fori_loop(0, peers // group, one_group, 0)

        def start(step, carry):
            patch(peer_at(step)[0], *buffers, me).start()
            return carry

        lax.fori_loop(1, peers, start, 0, unroll=peers <= 8)
        target[me] = source[me]

    def receive(buffers):
        def land(step, carry):
            other = peer_at(step)[0]
            patch(other, *buffers, other).wait_recv()
            return carry

        lax.fori_loop(1, peers, land, 0, unroll=peers <= 8)

    table_h = turned_table(phi_new[:layer_h], rows_h, hshape[2])
    post(to_torso, lambda peer: nodes.pick(table_h, peer))
    heart.pack(SWEEPS_H + 1, phi_new)
    heart.send(SWEEPS_H, SWEEPS_H + 1, 1)

    torso.begin(torso_phi[...], gains)
    partial = torso.complete(1, gains, end_gain)
    tpart[0] = partial
    receive(to_torso)
    summed = over_peers(
        lambda peer, carry: carry + voxels.place_at(arrived[peer], peer),
        jnp.zeros((rows, 2 * width), F32),
    )
    summed = summed[:, :width] + summed[:, width:]
    right = summed.reshape(layer, tshape[1], width) * right_t[...]
    right_t[...] = right

    coeffs = cheb_coeffs(SWEEPS_T)
    iterate = torso_phi[...]
    update = tpart[0] - iterate
    update = coeffs[0][1] * jnp.concatenate([update[:layer] + right, update[layer:]], axis=0)
    iterate = iterate + update
    for number in range(1, SWEEPS_T):
        torso.pack(number + 1, iterate)
        torso.send(number, number + 1, 1)
        torso.begin(iterate, gains)
        if number == 1:
            heart.begin(phi_h[...], which=1)
            loads[6].wait()
            loads[7].wait()
        count = states.shape[0]
        ionic(count * (number - 1) // (SWEEPS_T - 1), count * number // (SWEEPS_T - 1))
        torso.wait(number, number + 1, 1)
        residue = torso.complete(number + 1, gains, end_gain) - iterate
        residue = jnp.concatenate([residue[:layer] + right_t[...], residue[layer:]], axis=0)
        update = coeffs[number][0] * update + coeffs[number][1] * residue
        iterate = iterate + update
    table_t = turned_table(iterate[:layer], rows, width)
    post(
        to_heart, lambda peer: penalty * (arrived[peer] - voxels.pick(table_t, peer))
    )
    torso_out[...] = iterate
    stores[1].start()
    phi_new = phi_h[...]
    heart_phi[layer_h:] = phi_new[layer_h:]
    stores[2].start()
    heart.wait(SWEEPS_H, SWEEPS_H + 1, 1)
    lap_phi = diag * phi_new - heart.complete(SWEEPS_H + 1, which=1)
    new_membrane[...] = membrane[...] + time_step * (
        -intra_cond * (source_h[...] + lap_phi) - current_h[...]
    )
    stores[0].start()

    heart.finish(0, 0, 2)
    torso.finish(0, 0, 2)
    for number in range(1, SWEEPS_H + 1):
        heart.finish(number, number + 1, 1)
    for number in range(1, SWEEPS_T):
        torso.finish(number, number + 1, 1)

    receive(to_heart)
    flux = over_peers(
        lambda peer, carry: carry + nodes.place_at(came[peer], peer),
        jnp.zeros((rows_h, 2 * hshape[2]), F32),
    )
    flux = (flux[:, : hshape[2]] + flux[:, hshape[2] :]).reshape(layer_h, hshape[1], hshape[2])
    heart_phi[0:layer_h] = phi_new[:layer_h] - flux * (
        inverse[:layer_h] * (1.0 / (intra_cond + extra_cond))
    )
    stores[3].start()

    def settle(step, carry):
        other = peer_at(step)[0]
        patch(other, *to_torso, other).wait_send()
        patch(other, *to_heart, other).wait_send()
        return carry

    lax.fori_loop(1, peers, settle, 0, unroll=peers <= 8)
    for store in stores:
        store.wait()


def write_out(*refs):
    sources, targets, held, (sems,) = refs[:3], refs[3:6], refs[6:9], refs[9:]
    ins = [
        pltpu.make_async_copy(there, here, sems.at[0, number])
        for number, (there, here) in enumerate(zip(sources, held))
    ]
    outs = [
        pltpu.make_async_copy(here, there, sems.at[1, number])
        for number, (here, there) in enumerate(zip(held, targets))
    ]
    for copy in ins:
        copy.start()
    for copy, after in zip(ins, outs):
        copy.wait()
        after.start()
    for copy in outs:
        copy.wait()


def per_device(sizes, *args):
    peers, cap = args[8].shape[-2:]
    args = list(args)
    for number in (8, 10):
        args[number] = args[number].reshape(peers, cap)
    for number in (9, 11):
        args[number] = args[number].reshape(peers)
    hshape = args[1].shape
    tshape = args[4].shape
    hx, hy, hz = hshape
    tx, ty, tz = tshape
    hbm = pl.BlockSpec(memory_space=pltpu.HBM)
    in_smem = (3, 7, 9, 11)

    def grid_scratch(shape, slots, turns):
        nx, ny, nz = shape
        faces = [
            pltpu.VMEM((2, slots, ny, nz), F32),
            pltpu.VMEM((2, slots, nx, 1, nz), F32),
            pltpu.VMEM((2, slots, 1, nx * ny), F32),
        ]
        return (
            faces
            + faces
            + [
                pltpu.VMEM((nx, ny + 16, nz), F32),
                pltpu.SemaphoreType.DMA((turns, 3, 2)),
                pltpu.SemaphoreType.DMA((turns, 3, 2)),
            ]
        )

    staged = [
        pltpu.VMEM(hshape, F32),
        pltpu.VMEM(hshape, F32),
        pltpu.VMEM(tshape, F32),
        pltpu.SemaphoreType.DMA((4,)),
    ] + [
        (pltpu.SMEM if number in in_smem else pltpu.VMEM)(array.shape, array.dtype)
        for number, array in enumerate(args)
    ] + [pltpu.SemaphoreType.DMA((len(args),))]
    patches = [pltpu.VMEM((peers, 1, cap), F32)] * 4
    signals = [pltpu.SemaphoreType.DMA((peers,))] * 4
    rows_h = hx // 4 * hy
    rows = tx // 4 * ty
    work = [
        pltpu.VMEM((2,) + hshape, F32),
        pltpu.VMEM((1,) + tshape, F32),
        pltpu.VMEM(tshape, F32),
        pltpu.VMEM(hshape, F32),
        pltpu.VMEM(hshape, F32),
        pltpu.VMEM(hshape, F32),
        pltpu.VMEM((6, tx, ty, tz), F32),
        pltpu.VMEM((tx // 4, ty, tz), F32),
        pltpu.VMEM((rows, tz), F32),
        pltpu.VMEM((peers, rows_h, cap), BF16),
        pltpu.VMEM((peers, 1, cap), jnp.int32),
        pltpu.VMEM((peers, rows, cap), BF16),
        pltpu.VMEM((peers, 1, cap), jnp.int32),
    ]
    shapes = tuple(jax.ShapeDtypeStruct(shape, F32) for shape in (hshape, hshape, tshape))
    results = pl.pallas_call(
        functools.partial(kernel, sizes),
        out_shape=shapes,
        in_specs=[hbm] * len(args),
        out_specs=(hbm, hbm, hbm),
        scratch_shapes=staged
        + grid_scratch(hshape, SWEEPS_H + 2, SWEEPS_H + 1)
        + grid_scratch(tshape, SWEEPS_T + 1, SWEEPS_T)
        + patches
        + signals
        + work,
        compiler_params=pltpu.CompilerParams(
            collective_id=0, has_side_effects=True, vmem_limit_bytes=64 * 1024 * 1024
        ),
    )(*args)
    return pl.pallas_call(
        write_out,
        out_shape=shapes,
        in_specs=[hbm, hbm, hbm],
        out_specs=(hbm, hbm, hbm),
        scratch_shapes=[pltpu.VMEM(array.shape, F32) for array in shapes]
        + [pltpu.SemaphoreType.DMA((2, 3))],
        compiler_params=pltpu.CompilerParams(vmem_limit_bytes=64 * 1024 * 1024),
    )(*results)


def solution(mesh):
    sizes = (mesh.shape["grp"], mesh.shape["gx"], mesh.shape["gy"])
    placed = (
        P(None, "gx", "gy", "grp"),
        P("gx", "gy", "grp"),
        P("gx", "gy", "grp"),
        P(),
        P("gx", "gy", "grp"),
        P("gx", "gy", "grp"),
        P("gx", "gy", "grp"),
        P(),
        P("grp", "gx", "gy", None, None),
        P("grp", "gx", "gy", None),
        P("grp", "gx", "gy", None, None),
        P("grp", "gx", "gy", None),
    )
    return jax.shard_map(
        functools.partial(per_device, sizes),
        mesh=mesh,
        in_specs=placed,
        out_specs=(P("gx", "gy", "grp"), P("gx", "gy", "grp"), P("gx", "gy", "grp")),
        check_vma=False,
    )
```

```python
import functools

import jax
import jax.numpy as jnp
from jax import lax
from jax.experimental import pallas as pl
from jax.experimental.pallas import tpu as pltpu
from jax.sharding import PartitionSpec as P

LABELS = 4
SWEEPS_H = 3
SWEEPS_T = 4

time_step = 0.1
intra_cond = 0.25
extra_cond = 0.5
penalty = 2.0
cheb_low = 0.1
cheb_high = 2.0

MESH = pl.DeviceIdType.MESH
F32 = jnp.float32
BF16 = jnp.bfloat16


def cheb_coeffs(sweeps):
    centre = 0.5 * (cheb_high + cheb_low)
    half_width = 0.5 * (cheb_high - cheb_low)
    scaled = centre / half_width
    coeffs = [(0.0, 1.0 / centre)]
    rho_old = 1.0 / scaled
    for number in range(1, sweeps):
        rho_new = 1.0 / (2.0 * scaled - rho_old)
        coeffs.append((rho_new * rho_old, 2.0 * rho_new / half_width))
        rho_old = rho_new
    return coeffs


def harmonic(a, b):
    return 2.0 * a * b / (a + b)


def two_terms(values):
    high = values.astype(BF16)
    return high, (values - high.astype(F32)).astype(BF16)


class Grid:
    def __init__(self, shape, stage, landing, sends, recvs, ypad, place, partial):
        self.shape = shape
        self.stage = stage
        self.landing = landing
        self.sends = sends
        self.recvs = recvs
        self.ypad = ypad
        self.partial = partial
        self.place = place

    def clear_ends(self):
        nx, ny, nz = self.shape
        self.ypad[:, 7:8, :] = jnp.zeros((nx, 1, nz), F32)
        self.ypad[:, 8 + ny : 9 + ny, :] = jnp.zeros((nx, 1, nz), F32)
        for axis, (_, low, high) in enumerate(self.place):
            for side, (_, present) in enumerate((low, high)):
                if present is None:
                    continue

                @pl.when(jnp.logical_not(present))
                def _(axis=axis, side=side):
                    ref = self.landing[axis]
                    ref[side] = jnp.zeros(ref.shape[1:], F32)

    def pack(self, slot, field):
        nx, ny, nz = self.shape
        xs, ys, zs = self.stage
        xs[0, slot] = field[0]
        xs[1, slot] = field[nx - 1]
        ys[0, slot] = field[:, 0:1, :]
        ys[1, slot] = field[:, ny - 1 : ny, :]
        tiles = field.reshape(nx * ny // 8, 8, nz)
        lanes = lax.broadcasted_iota(jnp.int32, (8, nz), 1)
        pairs = lax.shift_right_logical((lanes + 1) & (nz - 1), 1)
        sums = [jnp.zeros((8, nz), F32) for _ in range(4)]
        for number in range(nx * ny // 8):
            tile = tiles[number]
            if number > 0:
                tile = pltpu.roll(tile, 2 * number, 1)
            sums[number % 4] = jnp.where(pairs == number, tile, sums[number % 4])
        both = (sums[0] + sums[1]) + (sums[2] + sums[3])
        zs[0, slot] = both
        zs[1, slot] = both

    def copies(self, turn, first, count):
        for axis, (name, low, high) in enumerate(self.place):
            for side, there in enumerate((low, high)):
                back = (high, low)[side]
                yield (
                    pltpu.make_async_remote_copy(
                        src_ref=self.stage[axis].at[side, pl.ds(first, count)],
                        dst_ref=self.landing[axis].at[1 - side, pl.ds(first, count)],
                        send_sem=self.sends.at[turn, axis, side],
                        recv_sem=self.recvs.at[turn, axis, 1 - side],
                        device_id={name: there[0]},
                        device_id_type=MESH,
                    ),
                    there[1],
                    back[1],
                )

    def send(self, turn, first, count):
        for copy, out, _ in self.copies(turn, first, count):
            if out is None:
                copy.start()
            else:
                pl.when(out)(copy.start)

    def wait(self, turn, first, count):
        for copy, _, back in self.copies(turn, first, count):
            if back is None:
                copy.wait_recv()
            else:
                pl.when(back)(copy.wait_recv)

    def finish(self, turn, first, count):
        for copy, out, _ in self.copies(turn, first, count):
            if out is None:
                copy.wait_send()
            else:
                pl.when(out)(copy.wait_send)

    def inside(self, field):
        nx, ny, nz = self.shape
        none = jnp.zeros((1, ny, nz), F32)
        below_x = jnp.concatenate([none, field[:-1]], axis=0)
        above_x = jnp.concatenate([field[1:], none], axis=0)
        self.ypad[:, 8 : 8 + ny, :] = field
        below_y = self.ypad[:, 7 : 7 + ny, :]
        above_y = self.ypad[:, 9 : 9 + ny, :]
        flat = field.reshape(nx * ny, nz)
        lanes = lax.broadcasted_iota(jnp.int32, (nx * ny, nz), 1)
        below_z = jnp.where(lanes == 0, 0.0, pltpu.roll(flat, 1, 1)).reshape(nx, ny, nz)
        above_z = jnp.where(lanes == nz - 1, 0.0, pltpu.roll(flat, nz - 1, 1)).reshape(nx, ny, nz)
        return below_x, above_x, below_y, above_y, below_z, above_z

    def begin(self, field, gains=None, which=0):
        parts = self.inside(field)
        if gains is not None:
            parts = [gains[number] * part for number, part in enumerate(parts)]
        self.partial[which] = total_of(parts)

    def ends(self, slot):
        nx, ny, nz = self.shape
        rz = self.landing[2]
        lanes = lax.broadcasted_iota(jnp.int32, (8, nz), 1)
        both = jnp.where(
            lanes & 1 == 0, pltpu.roll(rz[0, slot], 1, 1), pltpu.roll(rz[1, slot], nz - 1, 1)
        )
        tiles = [both] + [
            pltpu.roll(both, nz - 2 * number, 1) for number in range(1, nx * ny // 8)
        ]
        return jnp.concatenate(tiles, axis=0).reshape(nx, ny, nz)

    def complete(self, slot, gains=None, end_gain=None, which=0):
        nx, ny, nz = self.shape
        rx, ry, _ = self.landing
        ends = self.ends(slot)
        for side, at in ((0, 0), (1, nx - 1)):
            other = rx[side, slot]
            if gains is not None:
                other = gains[side, at] * other
            self.partial[which, at] = self.partial[which, at] + other
        for side, at in ((0, 0), (1, ny - 1)):
            other = ry[side, slot]
            if gains is not None:
                other = gains[2 + side, :, at : at + 1, :] * other
            self.partial[which, :, at : at + 1, :] = self.partial[which, :, at : at + 1, :] + other
        if end_gain is not None:
            ends = end_gain[...] * ends
        else:
            lanes = lax.broadcasted_iota(jnp.int32, (nx, ny, nz), 2)
            ends = jnp.where((lanes == 0) | (lanes == nz - 1), ends, 0.0)
        return self.partial[which] + ends

    def around(self, slot, field):
        nx, ny, nz = self.shape
        rx, ry, _ = self.landing
        below_x, above_x, below_y, above_y, below_z, above_z = self.inside(field)
        below_x = jnp.concatenate([rx[0, slot][None], below_x[1:]], axis=0)
        above_x = jnp.concatenate([above_x[:-1], rx[1, slot][None]], axis=0)
        rows = lax.broadcasted_iota(jnp.int32, (nx, ny, nz), 1)
        below_y = jnp.where(rows == 0, ry[0, slot], below_y)
        above_y = jnp.where(rows == ny - 1, ry[1, slot], above_y)
        lanes = lax.broadcasted_iota(jnp.int32, (nx, ny, nz), 2)
        ends = self.ends(slot)
        below_z = jnp.where(lanes == 0, ends, below_z)
        above_z = jnp.where(lanes == nz - 1, ends, above_z)
        return below_x, above_x, below_y, above_y, below_z, above_z


def total_of(parts):
    return ((parts[0] + parts[1]) + (parts[2] + parts[3])) + (parts[4] + parts[5])


def turned_table(layer, rows, width):
    high, low = two_terms(jnp.transpose(layer.reshape(rows, width)))
    return jnp.concatenate([high, low], axis=1)


class Patch:
    def __init__(self, nodes, counts, row_hots, columns, rows, width):
        self.nodes = nodes
        self.counts = counts
        self.row_hots = row_hots
        self.columns = columns
        self.rows = rows
        self.width = width
        self.cap = nodes.shape[1]

    def prepare(self, peer):
        index = self.nodes[pl.ds(peer, 1), :]
        slot_ids = lax.broadcasted_iota(jnp.int32, (1, self.cap), 1)
        index = jnp.where(slot_ids < self.counts[peer], index, -1)
        row_ids = lax.broadcasted_iota(jnp.int32, (self.rows, self.cap), 0)
        row = lax.shift_right_arithmetic(index, self.width.bit_length() - 1)
        self.row_hots[peer] = jnp.where(row_ids == row, 1.0, 0.0).astype(BF16)
        self.columns[peer] = index & (self.width - 1)

    def column_mask(self, peer):
        col_ids = lax.broadcasted_iota(jnp.int32, (self.width, self.cap), 0)
        return col_ids == self.columns[peer]

    def pick(self, table, peer):
        row_hot = self.row_hots[peer]
        chosen = jnp.dot(
            table, jnp.concatenate([row_hot, row_hot], axis=0), preferred_element_type=F32
        )
        return jnp.sum(jnp.where(self.column_mask(peer), chosen, 0.0), axis=0, keepdims=True)

    def weigh(self, peer):
        ones = jnp.where(self.column_mask(peer), 1.0, 0.0).astype(BF16)
        return lax.dot_general(
            self.row_hots[peer], ones, (((1,), (1,)), ((), ())), preferred_element_type=F32
        )

    def place_at(self, values, peer):
        mask = self.column_mask(peer)
        high = values.astype(BF16).astype(F32)
        low = values - high
        spread = jnp.concatenate(
            [jnp.where(mask, high, 0.0).astype(BF16), jnp.where(mask, low, 0.0).astype(BF16)],
            axis=0,
        )
        return lax.dot_general(
            self.row_hots[peer], spread, (((1,), (1,)), ((), ())), preferred_element_type=F32
        )


def kernel(
    sizes,
    states_in,
    membrane_in,
    phi_heart_in,
    ion_params_in,
    torso_phi_in,
    tissue_scale_in,
    labels_in,
    cond_table_in,
    send_node_in,
    send_count_in,
    recv_voxel_in,
    recv_count_in,
    new_membrane_out,
    heart_phi_out,
    torso_out_out,
    new_membrane, heart_phi, torso_out, store_sem,
    states, membrane, phi_heart, ion_params, torso_phi, tissue_scale, labels, cond_table,
    send_node, send_count, recv_voxel, recv_count, load_sem,
    hsx, hsy, hsz, hrx, hry, hrz, hypad, hsend, hrecv,
    tsx, tsy, tsz, trx, try_, trz, typad, tsend, trecv,
    sent, arrived, returned, came,
    out_sem, in_sem, back_sem, home_sem,
    hpart, tpart, end_gain, phi_h, source_h, current_h, gains, right_t, weight_t,
    rows_node, cols_node, rows_voxel, cols_voxel,
):
    n_grp, n_gx, n_gy = sizes
    peers = n_gx * n_gy
    group = 8 if peers % 8 == 0 else 1
    g = lax.axis_index("grp")
    i = lax.axis_index("gx")
    j = lax.axis_index("gy")
    me = i * n_gy + j
    hshape = membrane.shape
    tshape = torso_phi.shape

    sources = (
        (membrane_in, membrane), (phi_heart_in, phi_heart), (tissue_scale_in, tissue_scale),
        (labels_in, labels), (cond_table_in, cond_table), (torso_phi_in, torso_phi),
        (ion_params_in, ion_params), (states_in, states), (send_node_in, send_node),
        (send_count_in, send_count), (recv_voxel_in, recv_voxel), (recv_count_in, recv_count),
    )
    layer_h = hshape[0] // 4
    surface = pl.ds(0, layer_h)
    deep = pl.ds(layer_h, hshape[0] - layer_h)
    stores = [
        pltpu.make_async_copy(new_membrane, new_membrane_out, store_sem.at[0]),
        pltpu.make_async_copy(torso_out, torso_out_out, store_sem.at[1]),
        pltpu.make_async_copy(heart_phi.at[deep], heart_phi_out.at[deep], store_sem.at[2]),
        pltpu.make_async_copy(heart_phi.at[surface], heart_phi_out.at[surface], store_sem.at[3]),
    ]
    loads = [
        pltpu.make_async_copy(there, here, load_sem.at[number])
        for number, (there, here) in enumerate(sources)
    ]
    for load in loads:
        load.start()

    place = (
        ("gx", (lax.rem(i + n_gx - 1, n_gx), None), (lax.rem(i + 1, n_gx), None)),
        ("gy", (jnp.maximum(j - 1, 0), j > 0), (jnp.minimum(j + 1, n_gy - 1), j < n_gy - 1)),
        ("grp", (jnp.maximum(g - 1, 0), g > 0), (jnp.minimum(g + 1, n_grp - 1), g < n_grp - 1)),
    )
    heart = Grid(hshape, (hsx, hsy, hsz), (hrx, hry, hrz), hsend, hrecv, hypad, place, hpart)
    torso = Grid(tshape, (tsx, tsy, tsz), (trx, try_, trz), tsend, trecv, typad, place, tpart)
    heart.clear_ends()
    torso.clear_ends()

    def peer_at(step):
        other = lax.rem(me + step, peers)
        return other, {"gx": other // n_gy, "gy": lax.rem(other, n_gy)}

    barrier = pltpu.get_barrier_semaphore()

    def greet(step, carry):
        pl.semaphore_signal(barrier, inc=1, device_id=peer_at(step)[1], device_id_type=MESH)
        return carry

    lax.fori_loop(1, peers, greet, 0, unroll=peers <= 8)
    _, low_z, high_z = place[2]
    for there, present in (low_z, high_z):

        @pl.when(present)
        def _(there=there):
            pl.semaphore_signal(barrier, inc=1, device_id={"grp": there}, device_id_type=MESH)

    loads[0].wait()
    voltage = membrane[...]
    heart.pack(0, voltage)
    loads[1].wait()
    heart.pack(1, phi_heart[...])
    pl.semaphore_wait(
        barrier, peers - 1 + (g > 0).astype(jnp.int32) + (g < n_grp - 1).astype(jnp.int32)
    )
    heart.send(0, 0, 2)

    for load in loads[2:6]:
        load.wait()
    names = labels[...]
    table = jnp.where(names == 0, cond_table[0], 0.0)
    for number in range(1, LABELS):
        table = jnp.where(names == number, cond_table[number], table)
    conduct = tissue_scale[...] * table
    torso.pack(0, conduct)
    torso.pack(1, torso_phi[...])
    torso.send(0, 0, 2)

    def ionic(first, last):
        voltage = membrane[...]
        current = jnp.zeros(hshape, F32) if first == 0 else current_h[...]
        for state in range(first, last):
            line = jnp.zeros((1, 1, hshape[2]), F32)
            half_slope = 0.5 / (line + ion_params[1, state])
            decay = jnp.exp(line - time_step * ion_params[2, state])
            steady = 0.5 + 0.5 * jnp.tanh((voltage - ion_params[0, state]) * half_slope)
            gate = steady + (states[state].astype(F32) - steady) * decay
            current = current + ion_params[3, state] * gate * (voltage - ion_params[4, state])
        current_h[...] = current

    heart.begin(voltage, which=0)
    heart.begin(phi_heart[...], which=1)

    ny = lax.broadcasted_iota(jnp.int32, hshape, 1) + j * hshape[1]
    nz = lax.broadcasted_iota(jnp.int32, hshape, 2) + g * hshape[2]
    diag = (
        6.0
        - jnp.where(ny == 0, 1.0, 0.0)
        - jnp.where(ny == hshape[1] * n_gy - 1, 1.0, 0.0)
        - jnp.where(nz == 0, 1.0, 0.0)
        - jnp.where(nz == hshape[2] * n_grp - 1, 1.0, 0.0)
    )
    inverse = 1.0 / diag

    rows_h = layer_h * hshape[1]
    layer = tshape[0] // 4
    rows = layer * tshape[1]
    width = tshape[2]
    nodes = Patch(send_node, send_count, rows_node, cols_node, rows_h, hshape[2])
    voxels = Patch(recv_voxel, recv_count, rows_voxel, cols_voxel, rows, width)

    def over_peers(body, start):
        def one_group(number, carry):
            for offset in range(group):
                carry = body(number * group + offset, carry)
            return carry

        if peers == group:
            return one_group(0, start)
        return lax.fori_loop(0, peers // group, one_group, start)

    def indices():
        for load in loads[8:]:
            load.wait()

        def prepare(peer, carry):
            nodes.prepare(peer)
            voxels.prepare(peer)
            return carry + voxels.weigh(peer)

        weight_t[...] = penalty * over_peers(prepare, jnp.zeros((rows, width), F32))

    def conductances():
        torso.wait(0, 0, 2)
        faces = [harmonic(conduct, other) for other in torso.around(0, conduct)]
        weight = weight_t[...].reshape(layer, tshape[1], width)
        total = total_of(faces)
        total = jnp.concatenate([total[:layer] + weight, total[layer:]], axis=0)
        scale = 1.0 / total
        for number in range(6):
            gains[number] = faces[number] * scale
        lanes = lax.broadcasted_iota(jnp.int32, tshape, 2)
        end_gain[...] = jnp.where(
            lanes == 0, faces[4] * scale, jnp.where(lanes == width - 1, faces[5] * scale, 0.0)
        )
        right_t[...] = penalty * scale[:layer]

    heart.wait(0, 0, 2)
    lap_mem = diag * voltage - heart.complete(0, which=0)
    source_h[...] = lap_mem
    base = (-intra_cond / (intra_cond + extra_cond)) * lap_mem * inverse
    iterate = phi_heart[...]
    update = None
    for number, (carry_coef, resid_coef) in enumerate(cheb_coeffs(SWEEPS_H)):
        if number > 0:
            heart.wait(number, number + 1, 1)
        around = heart.complete(number + 1, which=1)
        residue = base - iterate + around * inverse
        update = resid_coef * residue if update is None else carry_coef * update + resid_coef * residue
        iterate = iterate + update
        if number < SWEEPS_H - 1:
            heart.pack(number + 2, iterate)
            heart.send(number + 1, number + 2, 1)
            heart.begin(iterate, which=1)
        if number == 0:
            indices()
        if number == 1:
            conductances()
    phi_new = iterate
    phi_h[...] = phi_new

    def patch(other, source, target, sends, recvs, mine):
        return pltpu.make_async_remote_copy(
            src_ref=source.at[other],
            dst_ref=target.at[mine],
            send_sem=sends.at[other],
            recv_sem=recvs.at[mine],
            device_id={"gx": other // n_gy, "gy": lax.rem(other, n_gy)},
            device_id_type=MESH,
        )

    to_torso = (sent, arrived, out_sem, in_sem)
    to_heart = (returned, came, back_sem, home_sem)

    def post(buffers, fill):
        source, target = buffers[:2]

        def one_group(number, carry):
            picked = [fill(number * group + offset) for offset in range(group)]
            for offset in range(group):
                source[number * group + offset] = picked[offset]
            return carry

        if peers == group:
            one_group(0, 0)
        else:
            lax.fori_loop(0, peers // group, one_group, 0)

        def start(step, carry):
            patch(peer_at(step)[0], *buffers, me).start()
            return carry

        lax.fori_loop(1, peers, start, 0, unroll=peers <= 8)
        target[me] = source[me]

    def receive(buffers):
        def land(step, carry):
            other = peer_at(step)[0]
            patch(other, *buffers, other).wait_recv()
            return carry

        lax.fori_loop(1, peers, land, 0, unroll=peers <= 8)

    table_h = turned_table(phi_new[:layer_h], rows_h, hshape[2])
    post(to_torso, lambda peer: nodes.pick(table_h, peer))
    heart.pack(SWEEPS_H + 1, phi_new)
    heart.send(SWEEPS_H, SWEEPS_H + 1, 1)

    torso.begin(torso_phi[...], gains)
    partial = torso.complete(1, gains, end_gain)
    tpart[0] = partial
    receive(to_torso)
    summed = over_peers(
        lambda peer, carry: carry + voxels.place_at(arrived[peer], peer),
        jnp.zeros((rows, 2 * width), F32),
    )
    summed = summed[:, :width] + summed[:, width:]
    right = summed.reshape(layer, tshape[1], width) * right_t[...]
    right_t[...] = right

    coeffs = cheb_coeffs(SWEEPS_T)
    iterate = torso_phi[...]
    update = tpart[0] - iterate
    update = coeffs[0][1] * jnp.concatenate([update[:layer] + right, update[layer:]], axis=0)
    iterate = iterate + update
    for number in range(1, SWEEPS_T):
        torso.pack(number + 1, iterate)
        torso.send(number, number + 1, 1)
        torso.begin(iterate, gains)
        if number == 1:
            heart.begin(phi_h[...], which=1)
            loads[6].wait()
            loads[7].wait()
        count = states.shape[0]
        ionic(count * (number - 1) // (SWEEPS_T - 1), count * number // (SWEEPS_T - 1))
        torso.wait(number, number + 1, 1)
        residue = torso.complete(number + 1, gains, end_gain) - iterate
        residue = jnp.concatenate([residue[:layer] + right_t[...], residue[layer:]], axis=0)
        update = coeffs[number][0] * update + coeffs[number][1] * residue
        iterate = iterate + update
    table_t = turned_table(iterate[:layer], rows, width)
    post(
        to_heart, lambda peer: penalty * (arrived[peer] - voxels.pick(table_t, peer))
    )
    torso_out[...] = iterate
    stores[1].start()
    phi_new = phi_h[...]
    heart_phi[layer_h:] = phi_new[layer_h:]
    stores[2].start()
    heart.wait(SWEEPS_H, SWEEPS_H + 1, 1)
    lap_phi = diag * phi_new - heart.complete(SWEEPS_H + 1, which=1)
    new_membrane[...] = membrane[...] + time_step * (
        -intra_cond * (source_h[...] + lap_phi) - current_h[...]
    )
    stores[0].start()

    heart.finish(0, 0, 2)
    torso.finish(0, 0, 2)
    for number in range(1, SWEEPS_H + 1):
        heart.finish(number, number + 1, 1)
    for number in range(1, SWEEPS_T):
        torso.finish(number, number + 1, 1)

    receive(to_heart)
    flux = over_peers(
        lambda peer, carry: carry + nodes.place_at(came[peer], peer),
        jnp.zeros((rows_h, 2 * hshape[2]), F32),
    )
    flux = (flux[:, : hshape[2]] + flux[:, hshape[2] :]).reshape(layer_h, hshape[1], hshape[2])
    heart_phi[0:layer_h] = phi_new[:layer_h] - flux * (
        inverse[:layer_h] * (1.0 / (intra_cond + extra_cond))
    )
    stores[3].start()

    def settle(step, carry):
        other = peer_at(step)[0]
        patch(other, *to_torso, other).wait_send()
        patch(other, *to_heart, other).wait_send()
        return carry

    lax.fori_loop(1, peers, settle, 0, unroll=peers <= 8)
    for store in stores:
        store.wait()


def write_out(*refs):
    sources, targets, held, (sems,) = refs[:3], refs[3:6], refs[6:9], refs[9:]
    ins = [
        pltpu.make_async_copy(there, here, sems.at[0, number])
        for number, (there, here) in enumerate(zip(sources, held))
    ]
    outs = [
        pltpu.make_async_copy(here, there, sems.at[1, number])
        for number, (here, there) in enumerate(zip(held, targets))
    ]
    for copy in ins:
        copy.start()
    for copy, after in zip(ins, outs):
        copy.wait()
        after.start()
    for copy in outs:
        copy.wait()


def per_device(sizes, *args):
    peers, cap = args[8].shape[-2:]
    args = list(args)
    for number in (8, 10):
        args[number] = args[number].reshape(peers, cap)
    for number in (9, 11):
        args[number] = args[number].reshape(peers)
    hshape = args[1].shape
    tshape = args[4].shape
    hx, hy, hz = hshape
    tx, ty, tz = tshape
    hbm = pl.BlockSpec(memory_space=pltpu.HBM)
    in_smem = (3, 7, 9, 11)

    def grid_scratch(shape, slots, turns):
        nx, ny, nz = shape
        faces = [
            pltpu.VMEM((2, slots, ny, nz), F32),
            pltpu.VMEM((2, slots, nx, 1, nz), F32),
            pltpu.VMEM((2, slots, 8, nz), F32),
        ]
        return (
            faces
            + faces
            + [
                pltpu.VMEM((nx, ny + 16, nz), F32),
                pltpu.SemaphoreType.DMA((turns, 3, 2)),
                pltpu.SemaphoreType.DMA((turns, 3, 2)),
            ]
        )

    staged = [
        pltpu.VMEM(hshape, F32),
        pltpu.VMEM(hshape, F32),
        pltpu.VMEM(tshape, F32),
        pltpu.SemaphoreType.DMA((4,)),
    ] + [
        (pltpu.SMEM if number in in_smem else pltpu.VMEM)(array.shape, array.dtype)
        for number, array in enumerate(args)
    ] + [pltpu.SemaphoreType.DMA((len(args),))]
    patches = [pltpu.VMEM((peers, 1, cap), F32)] * 4
    signals = [pltpu.SemaphoreType.DMA((peers,))] * 4
    rows_h = hx // 4 * hy
    rows = tx // 4 * ty
    work = [
        pltpu.VMEM((2,) + hshape, F32),
        pltpu.VMEM((1,) + tshape, F32),
        pltpu.VMEM(tshape, F32),
        pltpu.VMEM(hshape, F32),
        pltpu.VMEM(hshape, F32),
        pltpu.VMEM(hshape, F32),
        pltpu.VMEM((6, tx, ty, tz), F32),
        pltpu.VMEM((tx // 4, ty, tz), F32),
        pltpu.VMEM((rows, tz), F32),
        pltpu.VMEM((peers, rows_h, cap), BF16),
        pltpu.VMEM((peers, 1, cap), jnp.int32),
        pltpu.VMEM((peers, rows, cap), BF16),
        pltpu.VMEM((peers, 1, cap), jnp.int32),
    ]
    shapes = tuple(jax.ShapeDtypeStruct(shape, F32) for shape in (hshape, hshape, tshape))
    results = pl.pallas_call(
        functools.partial(kernel, sizes),
        out_shape=shapes,
        in_specs=[hbm] * len(args),
        out_specs=(hbm, hbm, hbm),
        scratch_shapes=staged
        + grid_scratch(hshape, SWEEPS_H + 2, SWEEPS_H + 1)
        + grid_scratch(tshape, SWEEPS_T + 1, SWEEPS_T)
        + patches
        + signals
        + work,
        compiler_params=pltpu.CompilerParams(
            collective_id=0, has_side_effects=True, vmem_limit_bytes=64 * 1024 * 1024
        ),
    )(*args)
    return pl.pallas_call(
        write_out,
        out_shape=shapes,
        in_specs=[hbm, hbm, hbm],
        out_specs=(hbm, hbm, hbm),
        scratch_shapes=[pltpu.VMEM(array.shape, F32) for array in shapes]
        + [pltpu.SemaphoreType.DMA((2, 3))],
        compiler_params=pltpu.CompilerParams(vmem_limit_bytes=64 * 1024 * 1024),
    )(*results)


def solution(mesh):
    sizes = (mesh.shape["grp"], mesh.shape["gx"], mesh.shape["gy"])
    placed = (
        P(None, "gx", "gy", "grp"),
        P("gx", "gy", "grp"),
        P("gx", "gy", "grp"),
        P(),
        P("gx", "gy", "grp"),
        P("gx", "gy", "grp"),
        P("gx", "gy", "grp"),
        P(),
        P("grp", "gx", "gy", None, None),
        P("grp", "gx", "gy", None),
        P("grp", "gx", "gy", None, None),
        P("grp", "gx", "gy", None),
    )
    return jax.shard_map(
        functools.partial(per_device, sizes),
        mesh=mesh,
        in_specs=placed,
        out_specs=(P("gx", "gy", "grp"), P("gx", "gy", "grp"), P("gx", "gy", "grp")),
        check_vma=False,
    )
```

```python
import functools

import jax
import jax.numpy as jnp
from jax import lax
from jax.experimental import pallas as pl
from jax.experimental.pallas import tpu as pltpu
from jax.sharding import PartitionSpec as P

LABELS = 4
SWEEPS_H = 3
SWEEPS_T = 4

time_step = 0.1
intra_cond = 0.25
extra_cond = 0.5
penalty = 2.0
cheb_low = 0.1
cheb_high = 2.0

MESH = pl.DeviceIdType.MESH
F32 = jnp.float32
BF16 = jnp.bfloat16


def cheb_coeffs(sweeps):
    centre = 0.5 * (cheb_high + cheb_low)
    half_width = 0.5 * (cheb_high - cheb_low)
    scaled = centre / half_width
    coeffs = [(0.0, 1.0 / centre)]
    rho_old = 1.0 / scaled
    for number in range(1, sweeps):
        rho_new = 1.0 / (2.0 * scaled - rho_old)
        coeffs.append((rho_new * rho_old, 2.0 * rho_new / half_width))
        rho_old = rho_new
    return coeffs


def harmonic(a, b):
    return 2.0 * a * b / (a + b)


def two_terms(values):
    high = values.astype(BF16)
    return high, (values - high.astype(F32)).astype(BF16)


class Grid:
    def __init__(self, shape, stage, landing, sends, recvs, ypad, place, partial):
        self.shape = shape
        self.stage = stage
        self.landing = landing
        self.sends = sends
        self.recvs = recvs
        self.ypad = ypad
        self.partial = partial
        self.place = place

    def clear_ends(self):
        nx, ny, nz = self.shape
        self.ypad[:, 7:8, :] = jnp.zeros((nx, 1, nz), F32)
        self.ypad[:, 8 + ny : 9 + ny, :] = jnp.zeros((nx, 1, nz), F32)
        for axis, (_, low, high) in enumerate(self.place):
            for side, (_, present) in enumerate((low, high)):
                if present is None:
                    continue

                @pl.when(jnp.logical_not(present))
                def _(axis=axis, side=side):
                    ref = self.landing[axis]
                    ref[side] = jnp.zeros(ref.shape[1:], F32)

    def pack(self, slot, field):
        nx, ny, nz = self.shape
        xs, ys, zs = self.stage
        xs[0, slot] = field[0]
        xs[1, slot] = field[nx - 1]
        ys[0, slot] = field[:, 0:1, :]
        ys[1, slot] = field[:, ny - 1 : ny, :]
        turned = jnp.transpose(field.reshape(nx * ny, nz))
        zs[0, slot] = turned[0:1, :]
        zs[1, slot] = turned[nz - 1 : nz, :]

    def copies(self, turn, first, count):
        for axis, (name, low, high) in enumerate(self.place):
            for side, there in enumerate((low, high)):
                back = (high, low)[side]
                yield (
                    pltpu.make_async_remote_copy(
                        src_ref=self.stage[axis].at[side, pl.ds(first, count)],
                        dst_ref=self.landing[axis].at[1 - side, pl.ds(first, count)],
                        send_sem=self.sends.at[turn, axis, side],
                        recv_sem=self.recvs.at[turn, axis, 1 - side],
                        device_id={name: there[0]},
                        device_id_type=MESH,
                    ),
                    there[1],
                    back[1],
                )

    def send(self, turn, first, count):
        for copy, out, _ in self.copies(turn, first, count):
            if out is None:
                copy.start()
            else:
                pl.when(out)(copy.start)

    def wait(self, turn, first, count):
        for copy, _, back in self.copies(turn, first, count):
            if back is None:
                copy.wait_recv()
            else:
                pl.when(back)(copy.wait_recv)

    def finish(self, turn, first, count):
        for copy, out, _ in self.copies(turn, first, count):
            if out is None:
                copy.wait_send()
            else:
                pl.when(out)(copy.wait_send)

    def inside(self, field):
        nx, ny, nz = self.shape
        none = jnp.zeros((1, ny, nz), F32)
        below_x = jnp.concatenate([none, field[:-1]], axis=0)
        above_x = jnp.concatenate([field[1:], none], axis=0)
        self.ypad[:, 8 : 8 + ny, :] = field
        below_y = self.ypad[:, 7 : 7 + ny, :]
        above_y = self.ypad[:, 9 : 9 + ny, :]
        flat = field.reshape(nx * ny, nz)
        lanes = lax.broadcasted_iota(jnp.int32, (nx * ny, nz), 1)
        below_z = jnp.where(lanes == 0, 0.0, pltpu.roll(flat, 1, 1)).reshape(nx, ny, nz)
        above_z = jnp.where(lanes == nz - 1, 0.0, pltpu.roll(flat, nz - 1, 1)).reshape(nx, ny, nz)
        return below_x, above_x, below_y, above_y, below_z, above_z

    def begin(self, field, gains=None, which=0):
        parts = self.inside(field)
        if gains is not None:
            parts = [gains[number] * part for number, part in enumerate(parts)]
        self.partial[which] = total_of(parts)

    def ends(self, slot):
        nx, ny, nz = self.shape
        rz = self.landing[2]
        depth = lax.broadcasted_iota(jnp.int32, (nz, nx * ny), 0)
        turned = jnp.where(depth == 0, rz[0, slot], jnp.where(depth == nz - 1, rz[1, slot], 0.0))
        return jnp.transpose(turned).reshape(nx, ny, nz)

    def complete(self, slot, gains=None, end_gain=None, which=0):
        nx, ny, nz = self.shape
        rx, ry, _ = self.landing
        ends = self.ends(slot)
        for side, at in ((0, 0), (1, nx - 1)):
            other = rx[side, slot]
            if gains is not None:
                other = gains[side, at] * other
            self.partial[which, at] = self.partial[which, at] + other
        for side, at in ((0, 0), (1, ny - 1)):
            other = ry[side, slot]
            if gains is not None:
                other = gains[2 + side, :, at : at + 1, :] * other
            self.partial[which, :, at : at + 1, :] = self.partial[which, :, at : at + 1, :] + other
        if end_gain is not None:
            ends = end_gain[...] * ends
        return self.partial[which] + ends

    def around(self, slot, field):
        nx, ny, nz = self.shape
        rx, ry, _ = self.landing
        below_x, above_x, below_y, above_y, below_z, above_z = self.inside(field)
        below_x = jnp.concatenate([rx[0, slot][None], below_x[1:]], axis=0)
        above_x = jnp.concatenate([above_x[:-1], rx[1, slot][None]], axis=0)
        rows = lax.broadcasted_iota(jnp.int32, (nx, ny, nz), 1)
        below_y = jnp.where(rows == 0, ry[0, slot], below_y)
        above_y = jnp.where(rows == ny - 1, ry[1, slot], above_y)
        lanes = lax.broadcasted_iota(jnp.int32, (nx, ny, nz), 2)
        ends = self.ends(slot)
        below_z = jnp.where(lanes == 0, ends, below_z)
        above_z = jnp.where(lanes == nz - 1, ends, above_z)
        return below_x, above_x, below_y, above_y, below_z, above_z


def total_of(parts):
    return ((parts[0] + parts[1]) + (parts[2] + parts[3])) + (parts[4] + parts[5])


def turned_table(layer, rows, width):
    high, low = two_terms(jnp.transpose(layer.reshape(rows, width)))
    return jnp.concatenate([high, low], axis=1)


class Patch:
    def __init__(self, nodes, counts, row_hots, columns, rows, width):
        self.nodes = nodes
        self.counts = counts
        self.row_hots = row_hots
        self.columns = columns
        self.rows = rows
        self.width = width
        self.cap = nodes.shape[1]

    def prepare(self, peer):
        index = self.nodes[pl.ds(peer, 1), :]
        slot_ids = lax.broadcasted_iota(jnp.int32, (1, self.cap), 1)
        index = jnp.where(slot_ids < self.counts[peer], index, -1)
        row_ids = lax.broadcasted_iota(jnp.int32, (self.rows, self.cap), 0)
        row = lax.shift_right_arithmetic(index, self.width.bit_length() - 1)
        self.row_hots[peer] = jnp.where(row_ids == row, 1.0, 0.0).astype(BF16)
        self.columns[peer] = index & (self.width - 1)

    def column_mask(self, peer):
        col_ids = lax.broadcasted_iota(jnp.int32, (self.width, self.cap), 0)
        return col_ids == self.columns[peer]

    def pick(self, table, peer):
        row_hot = self.row_hots[peer]
        chosen = jnp.dot(
            table, jnp.concatenate([row_hot, row_hot], axis=0), preferred_element_type=F32
        )
        return jnp.sum(jnp.where(self.column_mask(peer), chosen, 0.0), axis=0, keepdims=True)

    def weigh(self, peer):
        ones = jnp.where(self.column_mask(peer), 1.0, 0.0).astype(BF16)
        return lax.dot_general(
            self.row_hots[peer], ones, (((1,), (1,)), ((), ())), preferred_element_type=F32
        )

    def place_at(self, values, peer):
        mask = self.column_mask(peer)
        high = values.astype(BF16).astype(F32)
        low = values - high
        spread = jnp.concatenate(
            [jnp.where(mask, high, 0.0).astype(BF16), jnp.where(mask, low, 0.0).astype(BF16)],
            axis=0,
        )
        return lax.dot_general(
            self.row_hots[peer], spread, (((1,), (1,)), ((), ())), preferred_element_type=F32
        )


def kernel(
    sizes,
    states_in,
    membrane_in,
    phi_heart_in,
    ion_params_in,
    torso_phi_in,
    tissue_scale_in,
    labels_in,
    cond_table_in,
    send_node_in,
    send_count_in,
    recv_voxel_in,
    recv_count_in,
    new_membrane_out,
    heart_phi_out,
    torso_out_out,
    new_membrane, heart_phi, torso_out, store_sem,
    states, membrane, phi_heart, ion_params, torso_phi, tissue_scale, labels, cond_table,
    send_node, send_count, recv_voxel, recv_count, load_sem,
    hsx, hsy, hsz, hrx, hry, hrz, hypad, hsend, hrecv,
    tsx, tsy, tsz, trx, try_, trz, typad, tsend, trecv,
    sent, arrived, returned, came,
    out_sem, in_sem, back_sem, home_sem,
    hpart, tpart, end_gain, phi_h, source_h, current_h, gains, right_t, weight_t,
    rows_node, cols_node, rows_voxel, cols_voxel,
):
    n_grp, n_gx, n_gy = sizes
    peers = n_gx * n_gy
    group = 8 if peers % 8 == 0 else 1
    g = lax.axis_index("grp")
    i = lax.axis_index("gx")
    j = lax.axis_index("gy")
    me = i * n_gy + j
    hshape = membrane.shape
    tshape = torso_phi.shape

    sources = (
        (membrane_in, membrane), (phi_heart_in, phi_heart), (tissue_scale_in, tissue_scale),
        (labels_in, labels), (cond_table_in, cond_table), (torso_phi_in, torso_phi),
        (ion_params_in, ion_params), (states_in, states), (send_node_in, send_node),
        (send_count_in, send_count), (recv_voxel_in, recv_voxel), (recv_count_in, recv_count),
    )
    layer_h = hshape[0] // 4
    surface = pl.ds(0, layer_h)
    deep = pl.ds(layer_h, hshape[0] - layer_h)
    stores = [
        pltpu.make_async_copy(new_membrane, new_membrane_out, store_sem.at[0]),
        pltpu.make_async_copy(torso_out, torso_out_out, store_sem.at[1]),
        pltpu.make_async_copy(heart_phi.at[deep], heart_phi_out.at[deep], store_sem.at[2]),
        pltpu.make_async_copy(heart_phi.at[surface], heart_phi_out.at[surface], store_sem.at[3]),
    ]
    loads = [
        pltpu.make_async_copy(there, here, load_sem.at[number])
        for number, (there, here) in enumerate(sources)
    ]
    for load in loads:
        load.start()

    place = (
        ("gx", (lax.rem(i + n_gx - 1, n_gx), None), (lax.rem(i + 1, n_gx), None)),
        ("gy", (jnp.maximum(j - 1, 0), j > 0), (jnp.minimum(j + 1, n_gy - 1), j < n_gy - 1)),
        ("grp", (jnp.maximum(g - 1, 0), g > 0), (jnp.minimum(g + 1, n_grp - 1), g < n_grp - 1)),
    )
    heart = Grid(hshape, (hsx, hsy, hsz), (hrx, hry, hrz), hsend, hrecv, hypad, place, hpart)
    torso = Grid(tshape, (tsx, tsy, tsz), (trx, try_, trz), tsend, trecv, typad, place, tpart)
    heart.clear_ends()
    torso.clear_ends()

    def peer_at(step):
        other = lax.rem(me + step, peers)
        return other, {"gx": other // n_gy, "gy": lax.rem(other, n_gy)}

    barrier = pltpu.get_barrier_semaphore()

    def greet(step, carry):
        pl.semaphore_signal(barrier, inc=1, device_id=peer_at(step)[1], device_id_type=MESH)
        return carry

    lax.fori_loop(1, peers, greet, 0, unroll=peers <= 8)
    _, low_z, high_z = place[2]
    for there, present in (low_z, high_z):

        @pl.when(present)
        def _(there=there):
            pl.semaphore_signal(barrier, inc=1, device_id={"grp": there}, device_id_type=MESH)

    loads[0].wait()
    voltage = membrane[...]
    heart.pack(0, voltage)
    loads[1].wait()
    heart.pack(1, phi_heart[...])
    pl.semaphore_wait(
        barrier, peers - 1 + (g > 0).astype(jnp.int32) + (g < n_grp - 1).astype(jnp.int32)
    )
    heart.send(0, 0, 2)

    for load in loads[2:6]:
        load.wait()
    names = labels[...]
    table = jnp.where(names == 0, cond_table[0], 0.0)
    for number in range(1, LABELS):
        table = jnp.where(names == number, cond_table[number], table)
    conduct = tissue_scale[...] * table
    torso.pack(0, conduct)
    torso.pack(1, torso_phi[...])
    torso.send(0, 0, 2)

    def ionic(first, last):
        voltage = membrane[...]
        current = jnp.zeros(hshape, F32) if first == 0 else current_h[...]
        for state in range(first, last):
            line = jnp.zeros((1, 1, hshape[2]), F32)
            half_slope = 0.5 / (line + ion_params[1, state])
            decay = jnp.exp(line - time_step * ion_params[2, state])
            steady = 0.5 + 0.5 * jnp.tanh((voltage - ion_params[0, state]) * half_slope)
            gate = steady + (states[state].astype(F32) - steady) * decay
            current = current + ion_params[3, state] * gate * (voltage - ion_params[4, state])
        current_h[...] = current

    heart.begin(voltage, which=0)
    heart.begin(phi_heart[...], which=1)

    ny = lax.broadcasted_iota(jnp.int32, hshape, 1) + j * hshape[1]
    nz = lax.broadcasted_iota(jnp.int32, hshape, 2) + g * hshape[2]
    diag = (
        6.0
        - jnp.where(ny == 0, 1.0, 0.0)
        - jnp.where(ny == hshape[1] * n_gy - 1, 1.0, 0.0)
        - jnp.where(nz == 0, 1.0, 0.0)
        - jnp.where(nz == hshape[2] * n_grp - 1, 1.0, 0.0)
    )
    inverse = 1.0 / diag

    rows_h = layer_h * hshape[1]
    layer = tshape[0] // 4
    rows = layer * tshape[1]
    width = tshape[2]
    nodes = Patch(send_node, send_count, rows_node, cols_node, rows_h, hshape[2])
    voxels = Patch(recv_voxel, recv_count, rows_voxel, cols_voxel, rows, width)

    def over_peers(body, start):
        def one_group(number, carry):
            for offset in range(group):
                carry = body(number * group + offset, carry)
            return carry

        if peers == group:
            return one_group(0, start)
        return lax.fori_loop(0, peers // group, one_group, start)

    def indices():
        for load in loads[8:]:
            load.wait()

        def prepare(peer, carry):
            nodes.prepare(peer)
            voxels.prepare(peer)
            return carry + voxels.weigh(peer)

        weight_t[...] = penalty * over_peers(prepare, jnp.zeros((rows, width), F32))

    def conductances():
        torso.wait(0, 0, 2)
        faces = [harmonic(conduct, other) for other in torso.around(0, conduct)]
        weight = weight_t[...].reshape(layer, tshape[1], width)
        total = total_of(faces)
        total = jnp.concatenate([total[:layer] + weight, total[layer:]], axis=0)
        scale = 1.0 / total
        for number in range(6):
            gains[number] = faces[number] * scale
        lanes = lax.broadcasted_iota(jnp.int32, tshape, 2)
        end_gain[...] = jnp.where(
            lanes == 0, faces[4] * scale, jnp.where(lanes == width - 1, faces[5] * scale, 0.0)
        )
        right_t[...] = penalty * scale[:layer]

    heart.wait(0, 0, 2)
    lap_mem = diag * voltage - heart.complete(0, which=0)
    source_h[...] = lap_mem
    base = (-intra_cond / (intra_cond + extra_cond)) * lap_mem * inverse
    iterate = phi_heart[...]
    update = None
    for number, (carry_coef, resid_coef) in enumerate(cheb_coeffs(SWEEPS_H)):
        if number > 0:
            heart.wait(number, number + 1, 1)
        around = heart.complete(number + 1, which=1)
        residue = base - iterate + around * inverse
        update = resid_coef * residue if update is None else carry_coef * update + resid_coef * residue
        iterate = iterate + update
        if number < SWEEPS_H - 1:
            heart.pack(number + 2, iterate)
            heart.send(number + 1, number + 2, 1)
            heart.begin(iterate, which=1)
        if number == 0:
            indices()
        if number == 1:
            conductances()
    phi_new = iterate
    phi_h[...] = phi_new

    def patch(other, source, target, sends, recvs, mine):
        return pltpu.make_async_remote_copy(
            src_ref=source.at[other],
            dst_ref=target.at[mine],
            send_sem=sends.at[other],
            recv_sem=recvs.at[mine],
            device_id={"gx": other // n_gy, "gy": lax.rem(other, n_gy)},
            device_id_type=MESH,
        )

    to_torso = (sent, arrived, out_sem, in_sem)
    to_heart = (returned, came, back_sem, home_sem)

    def post(buffers, fill):
        source, target = buffers[:2]

        def start(step, carry):
            other = peer_at(step)[0]
            source[other] = fill(other)
            patch(other, *buffers, me).start()
            return carry

        lax.fori_loop(1, peers, start, 0, unroll=peers <= 8)
        target[me] = fill(me)

    def receive(buffers, spots, start):
        target = buffers[1]

        def land(step, carry):
            other = peer_at(step)[0]
            patch(other, *buffers, other).wait_recv()
            return carry + spots.place_at(target[other], other)

        own = start + spots.place_at(target[me], me)
        return lax.fori_loop(1, peers, land, own, unroll=peers <= 8)

    table_h = turned_table(phi_new[:layer_h], rows_h, hshape[2])
    post(to_torso, lambda peer: nodes.pick(table_h, peer))
    heart.pack(SWEEPS_H + 1, phi_new)
    heart.send(SWEEPS_H, SWEEPS_H + 1, 1)

    torso.begin(torso_phi[...], gains)
    partial = torso.complete(1, gains, end_gain)
    tpart[0] = partial
    summed = receive(to_torso, voxels, jnp.zeros((rows, 2 * width), F32))
    summed = summed[:, :width] + summed[:, width:]
    right = summed.reshape(layer, tshape[1], width) * right_t[...]
    right_t[...] = right

    coeffs = cheb_coeffs(SWEEPS_T)
    iterate = torso_phi[...]
    update = tpart[0] - iterate
    update = coeffs[0][1] * jnp.concatenate([update[:layer] + right, update[layer:]], axis=0)
    iterate = iterate + update
    for number in range(1, SWEEPS_T):
        torso.pack(number + 1, iterate)
        torso.send(number, number + 1, 1)
        torso.begin(iterate, gains)
        if number == 1:
            heart.begin(phi_h[...], which=1)
            loads[6].wait()
            loads[7].wait()
        count = states.shape[0]
        ionic(count * (number - 1) // (SWEEPS_T - 1), count * number // (SWEEPS_T - 1))
        torso.wait(number, number + 1, 1)
        residue = torso.complete(number + 1, gains, end_gain) - iterate
        residue = jnp.concatenate([residue[:layer] + right_t[...], residue[layer:]], axis=0)
        update = coeffs[number][0] * update + coeffs[number][1] * residue
        iterate = iterate + update
    table_t = turned_table(iterate[:layer], rows, width)
    post(
        to_heart, lambda peer: penalty * (arrived[peer] - voxels.pick(table_t, peer))
    )
    torso_out[...] = iterate
    stores[1].start()
    phi_new = phi_h[...]
    heart_phi[layer_h:] = phi_new[layer_h:]
    stores[2].start()
    heart.wait(SWEEPS_H, SWEEPS_H + 1, 1)
    lap_phi = diag * phi_new - heart.complete(SWEEPS_H + 1, which=1)
    new_membrane[...] = membrane[...] + time_step * (
        -intra_cond * (source_h[...] + lap_phi) - current_h[...]
    )
    stores[0].start()

    heart.finish(0, 0, 2)
    torso.finish(0, 0, 2)
    for number in range(1, SWEEPS_H + 1):
        heart.finish(number, number + 1, 1)
    for number in range(1, SWEEPS_T):
        torso.finish(number, number + 1, 1)

    flux = receive(to_heart, nodes, jnp.zeros((rows_h, 2 * hshape[2]), F32))
    flux = (flux[:, : hshape[2]] + flux[:, hshape[2] :]).reshape(layer_h, hshape[1], hshape[2])
    heart_phi[0:layer_h] = phi_new[:layer_h] - flux * (
        inverse[:layer_h] * (1.0 / (intra_cond + extra_cond))
    )
    stores[3].start()

    def settle(step, carry):
        other = peer_at(step)[0]
        patch(other, *to_torso, other).wait_send()
        patch(other, *to_heart, other).wait_send()
        return carry

    lax.fori_loop(1, peers, settle, 0, unroll=peers <= 8)
    for store in stores:
        store.wait()


def write_out(*refs):
    sources, targets, held, (sems,) = refs[:3], refs[3:6], refs[6:9], refs[9:]
    ins = [
        pltpu.make_async_copy(there, here, sems.at[0, number])
        for number, (there, here) in enumerate(zip(sources, held))
    ]
    outs = [
        pltpu.make_async_copy(here, there, sems.at[1, number])
        for number, (here, there) in enumerate(zip(held, targets))
    ]
    for copy in ins:
        copy.start()
    for copy, after in zip(ins, outs):
        copy.wait()
        after.start()
    for copy in outs:
        copy.wait()


def per_device(sizes, *args):
    peers, cap = args[8].shape[-2:]
    args = list(args)
    for number in (8, 10):
        args[number] = args[number].reshape(peers, cap)
    for number in (9, 11):
        args[number] = args[number].reshape(peers)
    hshape = args[1].shape
    tshape = args[4].shape
    hx, hy, hz = hshape
    tx, ty, tz = tshape
    hbm = pl.BlockSpec(memory_space=pltpu.HBM)
    in_smem = (3, 7, 9, 11)

    def grid_scratch(shape, slots, turns):
        nx, ny, nz = shape
        faces = [
            pltpu.VMEM((2, slots, ny, nz), F32),
            pltpu.VMEM((2, slots, nx, 1, nz), F32),
            pltpu.VMEM((2, slots, 1, nx * ny), F32),
        ]
        return (
            faces
            + faces
            + [
                pltpu.VMEM((nx, ny + 16, nz), F32),
                pltpu.SemaphoreType.DMA((turns, 3, 2)),
                pltpu.SemaphoreType.DMA((turns, 3, 2)),
            ]
        )

    staged = [
        pltpu.VMEM(hshape, F32),
        pltpu.VMEM(hshape, F32),
        pltpu.VMEM(tshape, F32),
        pltpu.SemaphoreType.DMA((4,)),
    ] + [
        (pltpu.SMEM if number in in_smem else pltpu.VMEM)(array.shape, array.dtype)
        for number, array in enumerate(args)
    ] + [pltpu.SemaphoreType.DMA((len(args),))]
    patches = [pltpu.VMEM((peers, 1, cap), F32)] * 4
    signals = [pltpu.SemaphoreType.DMA((peers,))] * 4
    rows_h = hx // 4 * hy
    rows = tx // 4 * ty
    work = [
        pltpu.VMEM((2,) + hshape, F32),
        pltpu.VMEM((1,) + tshape, F32),
        pltpu.VMEM(tshape, F32),
        pltpu.VMEM(hshape, F32),
        pltpu.VMEM(hshape, F32),
        pltpu.VMEM(hshape, F32),
        pltpu.VMEM((6, tx, ty, tz), F32),
        pltpu.VMEM((tx // 4, ty, tz), F32),
        pltpu.VMEM((rows, tz), F32),
        pltpu.VMEM((peers, rows_h, cap), BF16),
        pltpu.VMEM((peers, 1, cap), jnp.int32),
        pltpu.VMEM((peers, rows, cap), BF16),
        pltpu.VMEM((peers, 1, cap), jnp.int32),
    ]
    shapes = tuple(jax.ShapeDtypeStruct(shape, F32) for shape in (hshape, hshape, tshape))
    results = pl.pallas_call(
        functools.partial(kernel, sizes),
        out_shape=shapes,
        in_specs=[hbm] * len(args),
        out_specs=(hbm, hbm, hbm),
        scratch_shapes=staged
        + grid_scratch(hshape, SWEEPS_H + 2, SWEEPS_H + 1)
        + grid_scratch(tshape, SWEEPS_T + 1, SWEEPS_T)
        + patches
        + signals
        + work,
        compiler_params=pltpu.CompilerParams(
            collective_id=0, has_side_effects=True, vmem_limit_bytes=64 * 1024 * 1024
        ),
    )(*args)
    return pl.pallas_call(
        write_out,
        out_shape=shapes,
        in_specs=[hbm, hbm, hbm],
        out_specs=(hbm, hbm, hbm),
        scratch_shapes=[pltpu.VMEM(array.shape, F32) for array in shapes]
        + [pltpu.SemaphoreType.DMA((2, 3))],
        compiler_params=pltpu.CompilerParams(vmem_limit_bytes=64 * 1024 * 1024),
    )(*results)


def solution(mesh):
    sizes = (mesh.shape["grp"], mesh.shape["gx"], mesh.shape["gy"])
    placed = (
        P(None, "gx", "gy", "grp"),
        P("gx", "gy", "grp"),
        P("gx", "gy", "grp"),
        P(),
        P("gx", "gy", "grp"),
        P("gx", "gy", "grp"),
        P("gx", "gy", "grp"),
        P(),
        P("grp", "gx", "gy", None, None),
        P("grp", "gx", "gy", None),
        P("grp", "gx", "gy", None, None),
        P("grp", "gx", "gy", None),
    )
    return jax.shard_map(
        functools.partial(per_device, sizes),
        mesh=mesh,
        in_specs=placed,
        out_specs=(P("gx", "gy", "grp"), P("gx", "gy", "grp"), P("gx", "gy", "grp")),
        check_vma=False,
    )
```
